256 devices in a mesh: section: 16 (over y, x_hi, core), mp: 16 (over x_lo, z).
Axes of the slice: x: 4 (x_hi: 2, x_lo: 2; x = x_hi * 2 + x_lo), y: 4, z: 8, core: 2. Of those that a mesh axis runs over, the one named last changes fastest.
Arguments:
- states: bfloat16 [16, 512, 4096], P('section', 'mp'), may hold values from -6 to 6
- section_segs: int32 [16, 512], P('section'), may hold values from 0 to 3, never falling along the last dimension, each value on 1 to 256 neighbouring positions
- weights: bfloat16 [16, 4, 4096, 4096], P('section', None, None, 'mp'), may hold values from -1 to 1
- gains: float32 [16, 4096], P('section'), may hold values from 0.25 to 1.75
- memory: bfloat16 [512, 4096], P(('section', 'mp')), may hold values from -6 to 6
- memory_segs: int32 [512], replicated, may hold values from 0 to 3, never falling along the last dimension, each value on 1 to 256 neighbouring positions
- final_gain: float32 [4096], replicated, may hold values from 0.25 to 1.75
- embedding: bfloat16 [32768, 4096], P(('section', 'mp')), may hold values from -8 to 8
- targets: int32 [512], replicated, may hold values from 0 to 32767
Outputs:
- next_states: bfloat16 [16, 512, 4096], P('section', 'mp')
- loss: float32 [512], replicated
- embed_grad: float32 [32768, 4096], P(('section', 'mp'))
The draws below stay inside these ranges and needn't reach their ends.
All inputs are finite; a program needn't handle non-finite values.
Results may differ from the reference program's by a relative error of at most 0.029.
Values may be sent and summed in bfloat16 or wider, within the bound.
No kernel may reach another device: no remote copies, remote signals or barrier semaphores. Data moves between devices by JAX's collectives and lax.ppermute only.
A program may use at most 128 MiB of HBM per device.

```python
import math
import jax
import jax.numpy as jnp
import numpy as np
from jax import lax

D = 4096
HEAD_DIM = 64
VOCAB = 32768
TOK = 512
SEGS = 4
INNER = 4096
N_SECTION = 16
N_MP = 16


def clipped_normal(key, shape):
    return jnp.clip(jax.random.normal(key, shape, jnp.float32), -6.0, 6.0)


def draw_states(key, part):
    key = jax.random.fold_in(key, 11)
    noise = clipped_normal(jax.random.fold_in(key, 1), (N_SECTION, TOK, D))
    return noise.astype(jnp.bfloat16)


def draw_memory(key, part):
    key = jax.random.fold_in(key, 12)
    noise = clipped_normal(jax.random.fold_in(key, 1), (TOK, D))
    return noise.astype(jnp.bfloat16)


def draw_weights(key, part):
    key = jax.random.fold_in(key, 13)
    base = clipped_normal(jax.random.fold_in(key, 1), (N_SECTION, 4, D, INNER)) * (1.0 / D ** 0.5)
    return base.astype(jnp.bfloat16)


def draw_embedding(key, part):
    key = jax.random.fold_in(key, 14)
    base = clipped_normal(jax.random.fold_in(key, 1), (VOCAB, D)) * 0.05
    return base.astype(jnp.bfloat16)


def plant(result, own_key, least, top_value):
    longest = result.shape.index(max(result.shape))
    spots = []
    for shift in (0, 1):
        where = [jax.random.randint(jax.random.fold_in(own_key, axis), (), 0, length) for axis, length in enumerate(result.shape)]
        where[longest] = (where[longest] + shift) % result.shape[longest]
        spots.append(tuple(where))
    return result.at[spots[0]].set(least).at[spots[1]].set(top_value)


def rank_bounds(number_of, slope):
    portions = [(1 << 20) // math.isqrt(grade ** slope) + 1 for grade in range(1, number_of + 1)]
    width = 1 + sum(portions) // (1 << 30)
    return np.cumsum(np.array([max(1, weight // width) for weight in portions]))


def ranked(stream_key, dims, count, slope):
    table = rank_bounds(count, slope)
    lot = jax.random.randint(jax.random.fold_in(stream_key, 1), dims, 0, int(table[count - 1]))
    standing = jnp.searchsorted(jnp.asarray(table, jnp.int32), lot, side="right")
    return jax.random.permutation(jax.random.fold_in(stream_key, 2), count)[standing].astype(jnp.int32)


def length_profile(amount, total, most, slope):
    weights = [(1 << 20) // math.isqrt(grade ** slope) + 1 for grade in range(2, amount + 1)]
    surplus, holding = total - most - (amount - 1), [1] * (amount - 1)
    while surplus > 0:
        candidates = [i for i in range(amount - 1) if holding[i] < most]
        mass, budget = sum([weights[i] for i in candidates]), surplus
        for i in candidates:
            addition = min(most - holding[i], max(1, budget * weights[i] // mass), surplus)
            holding[i] = holding[i] + addition
            surplus = surplus - addition
    return np.array([most] + holding)


def ragged_sizes(own_key, number_of, total, limit, lean):
    if number_of == 2:
        one = jax.random.randint(own_key, (), max(1, total - limit), min(limit, total - 1) + 1)
        return jnp.stack([one, total - one])
    lengths = jnp.asarray(length_profile(number_of, total, limit, lean), jnp.int32)
    pairs = (number_of - 1) // 2
    source_of, sink = lengths[1:1 + 2 * pairs:2], lengths[2:2 + 2 * pairs:2]
    slack = jnp.minimum(source_of - 1, limit - sink)
    moved = jax.random.randint(jax.random.fold_in(own_key, 1), (pairs,), 0, 1 << 20) % (slack + 1)
    lengths = lengths.at[1:1 + 2 * pairs:2].set(source_of - moved).at[2:2 + 2 * pairs:2].set(sink + moved)
    return lengths[jax.random.permutation(jax.random.fold_in(own_key, 2), number_of)]


def setup_inputs(seed: int = 0) -> dict:
    key_of = jax.random.split(jax.random.key(seed), 10)
    return {
        "states": draw_states(jax.random.fold_in(key_of[9], 71), 0),
        "section_segs": jax.vmap(lambda own: jnp.searchsorted(jnp.cumsum(ragged_sizes(own, SEGS, TOK, TOK // 2, 2)), jnp.arange(TOK), side="right"))(jax.random.split(key_of[1], N_SECTION)).reshape((N_SECTION, TOK)).astype(jnp.int32),
        "weights": draw_weights(jax.random.fold_in(key_of[9], 71), 0),
        "gains": jnp.clip(1.0 + 0.15 * jax.random.normal(key_of[3], (N_SECTION, D), jnp.float32), 0.25, 1.75),
        "memory": draw_memory(jax.random.fold_in(key_of[9], 71), 0),
        "memory_segs": jnp.searchsorted(jnp.cumsum(ragged_sizes(key_of[5], SEGS, TOK, TOK // 2, 2)), jnp.arange(TOK), side="right").astype(jnp.int32),
        "final_gain": jnp.clip(1.0 + 0.15 * jax.random.normal(key_of[6], (D,), jnp.float32), 0.25, 1.75),
        "embedding": draw_embedding(jax.random.fold_in(key_of[9], 71), 0),
        "targets": plant(ranked(key_of[8], (TOK,), VOCAB, 2), jax.random.fold_in(key_of[8], 3), 0, VOCAB - 1).astype(jnp.int32),
    }


def norm_rows(rows, gain_row):
    as_float = rows.astype(jnp.float32)
    inverse = lax.rsqrt(lax.optimization_barrier(jnp.mean(as_float * as_float, axis=-1, keepdims=True)) + 1e-06)
    return as_float * inverse * gain_row

def attend(queries, key_rows, value_rows, allowed):
    query_count = queries.shape[0]
    key_count = key_rows.shape[0]
    heads_here = queries.shape[1] // HEAD_DIM
    query_heads = queries.astype(jnp.float32).reshape(query_count, heads_here, HEAD_DIM)
    key_heads = key_rows.astype(jnp.float32).reshape(key_count, heads_here, HEAD_DIM)
    value_heads = value_rows.astype(jnp.float32).reshape(key_count, heads_here, HEAD_DIM)
    scores = jnp.einsum('qhd,khd->hqk', query_heads, key_heads)
    masked = jnp.where(allowed[None], scores, -1e+30)
    highest = lax.optimization_barrier(jnp.max(masked, axis=-1, keepdims=True))
    powers = jnp.where(allowed[None], jnp.exp(masked - highest), 0.0)
    shares = (powers / lax.optimization_barrier(jnp.sum(powers, axis=-1, keepdims=True))).astype(jnp.bfloat16)
    mixed = jnp.einsum('hqk,khd->qhd', shares.astype(jnp.float32), value_heads)
    return mixed.reshape(query_count, heads_here * HEAD_DIM).astype(jnp.bfloat16)

def reference(states, section_segs, weights, gains, memory, memory_segs, final_gain, embedding, targets):
    section_count = states.shape[0]
    encoder_count = section_count // 2
    group_width = weights.shape[3] // N_MP
    outputs = []
    for section_index in range(section_count):
        current = states[section_index]
        layer_weight = weights[section_index]
        normed = norm_rows(current, gains[section_index]).astype(jnp.bfloat16)
        if section_index < encoder_count:
            key_source = normed
            key_segs = section_segs[section_index]
        else:
            key_source = memory
            key_segs = memory_segs
        queries = jnp.dot(normed, layer_weight[0], preferred_element_type=jnp.float32).astype(jnp.bfloat16)
        key_rows = jnp.dot(key_source, layer_weight[1], preferred_element_type=jnp.float32).astype(jnp.bfloat16)
        value_rows = jnp.dot(key_source, layer_weight[2], preferred_element_type=jnp.float32).astype(jnp.bfloat16)
        allowed = section_segs[section_index][:, None] == key_segs[None, :]
        attended = attend(queries, key_rows, value_rows, allowed)
        update = jnp.zeros((current.shape[0], current.shape[1]), jnp.float32)
        for group_index in range(N_MP):
            column_start = group_index * group_width
            partial_value = jnp.dot(attended[:, column_start:column_start + group_width], layer_weight[3][:, column_start:column_start + group_width].T, preferred_element_type=jnp.float32)
            rounded = lax.optimization_barrier(partial_value.astype(jnp.bfloat16))
            update = update + rounded.astype(jnp.float32)
        outputs.append((current.astype(jnp.float32) + update).astype(jnp.bfloat16))
    zeros_rows = jnp.zeros_like(outputs[0])
    shifted = [zeros_rows]
    for position in range(1, section_count):
        shifted.append(zeros_rows if position == encoder_count else outputs[position - 1])
    next_states = jnp.stack(shifted)
    final_rows = norm_rows(outputs[-1], final_gain).astype(jnp.bfloat16)
    logits = jnp.dot(final_rows, embedding.T, preferred_element_type=jnp.float32)
    highest = lax.optimization_barrier(jnp.max(logits, axis=-1))
    total = lax.optimization_barrier(jnp.sum(jnp.exp(logits - highest[:, None]), axis=-1))
    log_total = highest + jnp.log(total)
    picked = jnp.take_along_axis(logits, targets[:, None].astype(jnp.int32), axis=1)[:, 0]
    loss = log_total - picked
    owned = (jnp.arange(VOCAB, dtype=jnp.int32)[None, :] == targets[:, None]).astype(jnp.float32)
    slopes = (jnp.exp(logits - log_total[:, None]) - owned).astype(jnp.bfloat16)
    embed_grad = jnp.dot(slopes.T, final_rows, preferred_element_type=jnp.float32)
    return (next_states, loss, embed_grad)
```

```python
import jax
import jax.numpy as jnp
from jax import lax
from jax.sharding import Mesh
from jax.sharding import PartitionSpec as P

HEAD_DIM = 64
SECTION = ("y", "xh", "c")
MP = ("xl", "z")


def shift(block, axis, distance):
    count = lax.axis_size(axis)
    return lax.ppermute(block, axis, [(i, (i + distance) % count) for i in range(count)])


def norm_rows(rows, gain_row):
    as_float = rows.astype(jnp.float32)
    inverse = lax.rsqrt(jnp.mean(as_float * as_float, axis=-1, keepdims=True) + 1e-06)
    return as_float * inverse * gain_row


def gather_ring(block):
    pair = jnp.concatenate([block, shift(block, "xl", 1)], axis=0)
    half = pair.shape[1] // 2
    up, down = [pair], [pair]
    for _ in range(3):
        up.append(shift(up[-1], "z", 1))
        down.append(shift(down[-1], "z", -1))
    left = shift(up[3][:, :half], "z", 1)
    right = shift(down[3][:, half:], "z", -1)
    return jnp.concatenate(up + down[1:] + [jnp.concatenate([left, right], axis=1)], axis=0)


def relative(values):
    z = lax.axis_index("z")
    flipped = jnp.where(lax.axis_index("xl") == 1, values[::-1], values)
    rolled = lax.dynamic_slice_in_dim(jnp.concatenate([flipped, flipped], axis=1), z, 8, axis=1)
    ordered = jnp.concatenate([rolled[:, :1], rolled[:, :4:-1], rolled[:, 1:5]], axis=1)
    return jnp.swapaxes(ordered, 0, 1)


def absolute(values):
    z = lax.axis_index("z")
    ordered = jnp.swapaxes(values, 0, 1)
    rolled = jnp.concatenate([ordered[:, :1], ordered[:, 4:], ordered[:, 3:0:-1]], axis=1)
    unrolled = lax.dynamic_slice_in_dim(jnp.concatenate([rolled, rolled], axis=1), 8 - z, 8, axis=1)
    return jnp.where(lax.axis_index("xl") == 1, unrolled[::-1], unrolled)


def scatter_ring(parts):
    count = parts.shape[0] // 8
    half = parts.shape[1] // 2
    block = [parts[i * count : (i + 1) * count] for i in range(8)]
    as_float = lambda a: a.astype(jnp.float32)
    up = shift(block[7][:, :half], "z", 1)
    down = shift(block[7][:, half:], "z", -1)
    up = jnp.concatenate([as_float(up) + as_float(block[6][:, :half]), as_float(block[6][:, half:])], axis=1)
    down = jnp.concatenate([as_float(block[3][:, :half]), as_float(down) + as_float(block[3][:, half:])], axis=1)
    up = shift(up.astype(parts.dtype), "z", 1)
    down = shift(down.astype(parts.dtype), "z", -1)
    for step in (2, 1):
        up = shift((as_float(up) + as_float(block[3 + step])).astype(parts.dtype), "z", 1)
        down = shift((as_float(down) + as_float(block[step])).astype(parts.dtype), "z", -1)
    total = as_float(block[0]) + as_float(up) + as_float(down)
    rows = count // 2
    other = shift(total[rows:].astype(parts.dtype), "xl", 1)
    return total[:rows] + as_float(other)


def gather_memory(memory):
    rows = jnp.concatenate([memory, shift(memory, "xh", 1)], axis=0)
    rows = jnp.concatenate([rows] + [shift(rows, "y", d) for d in (1, 2, 3)], axis=0)
    mine = lax.all_gather(rows, MP, axis=0, tiled=True)
    return jnp.concatenate([mine, shift(mine, "c", 1)], axis=0)


def memory_order(segs):
    values = segs.reshape(4, 2, 2, 16, 2)
    values = lax.dynamic_slice_in_dim(jnp.concatenate([values, values], axis=0), lax.axis_index("y"), 4, axis=0)
    values = jnp.concatenate([values[:1], values[:0:-1]], axis=0)
    values = jnp.where(lax.axis_index("xh") == 1, values[:, ::-1], values)
    values = jnp.where(lax.axis_index("c") == 1, values[:, :, ::-1], values)
    return values.transpose(2, 3, 0, 1, 4).reshape(-1)


def attend(queries, key_rows, value_rows, allowed):
    query_count = queries.shape[0]
    key_count = key_rows.shape[0]
    heads_here = queries.shape[1] // HEAD_DIM
    query_heads = queries.reshape(query_count, heads_here, HEAD_DIM)
    key_heads = key_rows.reshape(key_count, heads_here, HEAD_DIM)
    value_heads = value_rows.reshape(key_count, heads_here, HEAD_DIM)
    scores = jnp.einsum("qhd,khd->hqk", query_heads, key_heads, preferred_element_type=jnp.float32)
    masked = jnp.where(allowed[None], scores, -1e30)
    highest = jnp.max(masked, axis=-1, keepdims=True)
    powers = jnp.where(allowed[None], jnp.exp(masked - highest), 0.0)
    shares = (powers / jnp.sum(powers, axis=-1, keepdims=True)).astype(jnp.bfloat16)
    mixed = jnp.einsum("hqk,khd->qhd", shares, value_heads, preferred_element_type=jnp.float32)
    return mixed.reshape(query_count, heads_here * HEAD_DIM).astype(jnp.bfloat16)


def spread_final(rows):
    half = rows.shape[0] // 2
    plane = lax.axis_index("y") * 2 + lax.axis_index("xh")
    moved = lax.ppermute(rows[:half], "c", [(1, 0)])
    mine = jnp.where(lax.axis_index("c") == 1, rows[half:], moved)
    moved = lax.ppermute(mine, ("y", "xh"), [(7, 6)])
    mine = jnp.where(plane == 6, moved, mine)
    first = lax.ppermute(mine, ("y", "xh"), [(7, 5), (6, 4)])
    second = lax.ppermute(mine, ("y", "xh"), [(7, 1), (6, 0)])
    third = lax.ppermute(mine, ("y", "xh"), [(7, 3), (6, 2)])
    return jnp.where(plane >= 6, mine, jnp.where(plane >= 4, first, jnp.where(plane < 2, second, third)))


def combine(stats, axis):
    count = lax.axis_size(axis)
    every = lax.all_to_all(jnp.broadcast_to(stats[None], (count,) + stats.shape), axis, 0, 0)
    highest = jnp.max(every[:, 0], axis=0)
    total = jnp.sum(every[:, 1] * jnp.exp(every[:, 0] - highest), axis=0)
    return jnp.stack([highest, total, jnp.sum(every[:, 2], axis=0)])


def per_device(
    states, section_segs, weights, gains, memory, memory_segs, final_gain, embedding, targets
):
    section_index = lax.axis_index(SECTION)
    current = states[0]
    layer_weight = weights[0]
    normed = gather_ring(norm_rows(current, gains[0]).astype(jnp.bfloat16))
    remembered = gather_memory(memory)
    query_segs = relative(section_segs[0].reshape(2, 8, 32)).reshape(-1)
    encoding = section_index < 8
    key_source = jnp.where(encoding, normed, remembered)
    key_segs = jnp.where(encoding, query_segs, memory_order(memory_segs))
    queries = jnp.dot(normed, layer_weight[0], preferred_element_type=jnp.float32).astype(jnp.bfloat16)
    key_rows = jnp.dot(key_source, layer_weight[1], preferred_element_type=jnp.float32).astype(jnp.bfloat16)
    value_rows = jnp.dot(key_source, layer_weight[2], preferred_element_type=jnp.float32).astype(jnp.bfloat16)
    allowed = query_segs[:, None] == key_segs[None, :]
    attended = attend(queries, key_rows, value_rows, allowed)
    partials = lax.dot_general(
        attended, layer_weight[3], (((1,), (1,)), ((), ())), preferred_element_type=jnp.float32
    ).astype(jnp.bfloat16)
    summed = scatter_ring(partials)
    updated = (current.astype(jnp.float32) + summed).astype(jnp.bfloat16)
    final_part = norm_rows(updated, final_gain).astype(jnp.bfloat16)
    mine = gather_ring(spread_final(final_part))
    swapped = shift(mine, "c", 1)
    next_states = lax.ppermute(updated[None], SECTION, [(i, i + 1) for i in range(15) if i != 7])

    final_all = jnp.concatenate([mine, swapped], axis=0)
    core = lax.axis_index("c")
    def to_tokens(value):
        value = jnp.where(core == 1, value[::-1], value)
        return jnp.stack([absolute(value[0]), absolute(value[1])], axis=2).reshape(-1)

    def to_rows(value):
        halves = value.reshape(2, 8, 2, 16)
        halves = jnp.where(core == 1, halves[:, :, ::-1], halves)
        return jnp.stack([relative(halves[:, :, 0]), relative(halves[:, :, 1])]).reshape(-1)

    row_targets = to_rows(targets)
    logits = lax.dot_general(
        embedding, final_all, (((1,), (1,)), ((), ())), preferred_element_type=jnp.float32
    )
    vocab_local = embedding.shape[0]
    vocab_start = (section_index * 16 + lax.axis_index(MP)) * vocab_local
    owned = (row_targets - vocab_start)[None, :] == jnp.arange(vocab_local, dtype=jnp.int32)[:, None]
    local_max = jnp.max(logits, axis=0)
    local_sum = jnp.sum(jnp.exp(logits - local_max), axis=0)
    picked = jnp.sum(jnp.where(owned, logits, 0.0), axis=0)
    stats = jnp.stack([local_max, local_sum, picked]).reshape(3, 2, 8, 2, 16)

    stats = jnp.stack([to_tokens(stats[i]) for i in range(3)])
    stats = combine(combine(stats, MP), SECTION)
    log_total = stats[0] + jnp.log(stats[1])
    loss = log_total - stats[2]
    row_total = to_rows(log_total)
    slopes = (jnp.exp(logits - row_total[None, :]) - owned.astype(jnp.float32)).astype(jnp.bfloat16)
    embed_grad = jnp.dot(slopes, final_all, preferred_element_type=jnp.float32)
    return (next_states, loss, embed_grad)


def solution(mesh):
    fine = Mesh(mesh.devices.reshape(4, 2, 2, 2, 8), ("y", "xh", "c", "xl", "z"))
    everything = P(SECTION + MP, None)
    placed = (
        P(SECTION, MP, None),
        P(SECTION, None),
        P(SECTION, None, None, MP),
        P(SECTION, None),
        everything,
        P(),
        P(),
        everything,
        P(),
    )
    return jax.shard_map(
        per_device,
        mesh=fine,
        in_specs=placed,
        out_specs=(P(SECTION, MP, None), P(), everything),
        check_vma=False,
    )
```

```python
import functools

import jax
import jax.numpy as jnp
from jax import lax
from jax.experimental import pallas as pl
from jax.experimental.pallas import tpu as pltpu
from jax.sharding import Mesh
from jax.sharding import PartitionSpec as P

HEAD_DIM = 64
SECTION = ("y", "xh", "c")
MP = ("xl", "z")


def shift(block, axis, distance):
    count = lax.axis_size(axis)
    return lax.ppermute(block, axis, [(i, (i + distance) % count) for i in range(count)])


def norm_rows(rows, gain_row):
    as_float = rows.astype(jnp.float32)
    inverse = lax.rsqrt(jnp.mean(as_float * as_float, axis=-1, keepdims=True) + 1e-06)
    return as_float * inverse * gain_row


together = lax.optimization_barrier


def inner(block):
    return lax.ppermute(block, "z", [(i, i ^ 1) for i in range(8)])


def outer(block):
    return lax.ppermute(block, "z", [(i, (i + 1) % 8 if i % 2 else (i - 1) % 8) for i in range(8)])


def across(block):
    return shift(block, "xl", 1)


def gather_blocks(block, beside=lambda step, known, blocks: known):
    half = block.shape[1] // 2
    own, other, fresh = [block], [], [block]
    ahead, behind = block, block
    side, pending = (), ()
    for step in range(4):
        if step < 3:
            behind, ahead = outer(ahead), inner(behind)
            arrived = (ahead, behind)
        else:
            arrived = (inner(behind[:, :half]), outer(ahead[:, half:]))
        crossed = tuple(across(b) for b in fresh)
        side = beside(step, side, list(zip(own, other + list(pending))))
        arrived, pending, side = together((arrived, pending, side))
        if step < 3:
            ahead, behind = arrived
        own += arrived
        other += pending
        pending, fresh = crossed, arrived
    other += pending
    other += [across(b) for b in fresh]
    return list(zip(own, other)), side


def scatter_blocks(own, other):
    half = own[0].shape[1] // 2
    as_float = lambda a: a.astype(jnp.float32)
    narrow = lambda a: a.astype(jnp.bfloat16)
    other = list(other)
    far = narrow(as_float(own[7]) + as_float(across(other[7])))
    pending = (across(other[6]), across(other[5]))
    far, other[4], other[3] = together((far, other[4], other[3]))
    moved = (inner(far[:, :half]), outer(far[:, half:]))
    crossed = (across(other[4]), across(other[3]))
    (left, right), (one, two), other[2], other[1] = together((moved, pending, other[2], other[1]))
    minus = as_float(own[6]) + as_float(one)
    plus = as_float(own[5]) + as_float(two)
    up = narrow(jnp.concatenate([minus[:, :half] + as_float(left), minus[:, half:]], axis=1))
    down = narrow(jnp.concatenate([plus[:, :half], plus[:, half:] + as_float(right)], axis=1))
    for step in (2, 1):
        moved, pending = (outer(up), inner(down)), crossed
        if step == 2:
            crossed = (across(other[2]), across(other[1]))
        else:
            crossed = (across(other[0]),)
        (up, down), (one, two), other[0] = together((moved, pending, other[0]))
        up, down = (
            narrow(as_float(own[2 * step]) + as_float(one) + as_float(down)),
            narrow(as_float(own[2 * step - 1]) + as_float(two) + as_float(up)),
        )
    up, down = outer(up), inner(down)
    return as_float(own[0]) + as_float(crossed[0]) + as_float(up) + as_float(down)


def pick(values, index):
    places = jnp.arange(values.shape[0], dtype=jnp.int32)
    return jnp.sum(jnp.where(index[:, None] == places[None, :], values[None, :], 0), axis=1)


def memory_rows():
    at = jnp.arange(512, dtype=jnp.int32)
    near = at < 320
    core = lax.axis_index("c") ^ jnp.where(near, at // 160, (at - 320) // 96)
    column = lax.axis_index("xl") ^ jnp.where(near, at // 80 % 2, (at - 320) // 48 % 2)
    place = jnp.where(near, at % 80 // 16, 5 + (at - 320) % 48 // 16)
    z = lax.axis_index("z")
    ahead = jnp.where(place % 2 == 1, (place + 1) // 2, -(place // 2)) * (1 - 2 * (z % 2))
    z = (z + 8 + ahead) % 8
    y = (lax.axis_index("y") + 4 - at // 4 % 4) % 4
    xh = lax.axis_index("xh") ^ (at // 2 % 2)
    return (y * 4 + xh * 2 + core) * 32 + (column * 8 + z) * 2 + at % 2


def memory_kernel(places, *refs):
    count = len(places)
    blocks, out, held, in_sems, out_sem = refs[:count], *refs[count:]
    copies = []
    for i, (row, column, width) in enumerate(places):
        target = held.at[pl.ds(row, 16), pl.ds(column, width)]
        copies.append(pltpu.make_async_copy(blocks[i].at[32:], target, in_sems.at[i]))
    for copy in copies:
        copy.start()
    for copy in copies:
        copy.wait()
    copy = pltpu.make_async_copy(held, out, out_sem)
    copy.start()
    copy.wait()


def memory_of(blocks):
    width = blocks[0][0].shape[1]
    whole = [i for i, pair in enumerate(blocks) if pair[0].shape[1] == width]
    rows = 16 * (len(whole) + (len(blocks) - len(whole)) // 2)
    places, flat = [], []
    for other in range(2):
        for i, pair in enumerate(blocks):
            part = 0 if i in whole else i - len(whole)
            place = i if i in whole else len(whole)
            flat.append(pair[other])
            places.append((rows * other + 16 * place, part * width // 2, pair[other].shape[1]))
    anywhere = pl.BlockSpec(memory_space=pl.ANY)
    return pl.pallas_call(
        functools.partial(memory_kernel, places),
        out_shape=jax.ShapeDtypeStruct((2 * rows, width), flat[0].dtype),
        in_specs=[anywhere] * len(flat),
        out_specs=anywhere,
        scratch_shapes=[
            pltpu.VMEM((2 * rows, width), flat[0].dtype),
            pltpu.SemaphoreType.DMA((len(flat),)),
            pltpu.SemaphoreType.DMA,
        ],
        compiler_params=pltpu.CompilerParams(vmem_limit_bytes=60 * 1024 * 1024),
        cost_estimate=pl.CostEstimate(flops=0, bytes_accessed=4_000_000, transcendentals=0),
    )(*flat)


def layer_kernel(*refs):
    place = refs[0]
    pairs = refs[1:19]
    memory_refs = refs[19:23]
    weight, query_segs, key_segs = refs[23:26]
    outs = refs[26:42]
    source, held, total, attended, partial, in_sems, memory_sems, weight_sems, out_sems = refs[42:]
    z, sign, column, decoding = place[0], place[1], place[2], place[3]
    half = source.shape[2] // 2
    tokens, width = attended.shape
    chunk = 1024
    chunks = held.shape[1] // chunk
    halves = [pl.ds(0, half), pl.ds(half, half)]

    def row(offset, other):
        col = column if other == 0 else 1 - column
        return pl.multiple_of((lax.rem(z + 8 + offset, 8) * 2 + col) * 32, 32)

    offsets = [0, sign, -sign, 2 * sign, -2 * sign, 3 * sign, -3 * sign, 4]

    def pair_copy(i, other, side):
        rows = pl.ds(row(offsets[i], other), 32)
        block = pairs[2 * (i + side) + other].at[:32] if i == 7 else pairs[2 * i + other].at[:32, halves[side]]
        return pltpu.make_async_copy(block, source.at[0, rows, halves[side]], in_sems.at[side, 2 * i + other])

    def weight_copy(j, k):
        rows = pl.ds(k * chunk, chunk)
        return pltpu.make_async_copy(weight.at[j, rows], held.at[j, rows], weight_sems.at[j, k])

    def memory_copy(i, side):
        count = memory_refs[i].shape[0]
        first = sum(memory_refs[before].shape[0] for before in range(i))
        return pltpu.make_async_copy(
            memory_refs[i].at[:, halves[side]], source.at[1, pl.ds(first, count), halves[side]], memory_sems.at[side, i]
        )

    pair_copies = [[pair_copy(i, other, side) for i in range(8) for other in range(2)] for side in range(2)]
    memory_copies = [[memory_copy(i, side) for i in range(4)] for side in range(2)]
    for side in range(2):
        for copy in pair_copies[side]:
            copy.start()

        @pl.when(decoding == 1)
        def _():
            for copy in memory_copies[side]:
                copy.start()

        for k in range(side * chunks // 2, (side + 1) * chunks // 2):
            for j in range(3):
                weight_copy(j, k).start()
    for k in range(chunks):
        weight_copy(3, k).start()

    for k in range(chunks):
        if k % (chunks // 2) == 0:
            side = k // (chunks // 2)
            for copy in pair_copies[side]:
                copy.wait()

            @pl.when(decoding == 1)
            def _():
                for copy in memory_copies[side]:
                    copy.wait()

        for j in range(3):
            weight_copy(j, k).wait()
        columns = pl.ds(k * chunk, chunk)
        for j in range(3):
            rows = source[0, :, columns] if j == 0 else source[decoding, :, columns]
            part = jnp.dot(rows, held[j, columns, :], preferred_element_type=jnp.float32)
            if k == 0:
                total[j] = part
            else:
                total[j] += part

    allowed = query_segs[...] == key_segs[...]
    lane = lax.broadcasted_iota(jnp.int32, (1, 2 * HEAD_DIM), 1)
    for two in range(width // (2 * HEAD_DIM)):
        lanes = pl.ds(two * 2 * HEAD_DIM, 2 * HEAD_DIM)
        queries = total[0, :, lanes].astype(jnp.bfloat16)
        key_rows = total[1, :, lanes].astype(jnp.bfloat16)
        value_rows = total[2, :, lanes].astype(jnp.bfloat16)
        mixed = None
        for head in range(2):
            here = (lane // HEAD_DIM) == head
            one = jnp.where(here, queries, jnp.zeros_like(queries))
            scores = lax.dot_general(
                one, key_rows, (((1,), (1,)), ((), ())), preferred_element_type=jnp.float32
            )
            masked = jnp.where(allowed, scores, -1e30)
            highest = jnp.max(masked, axis=-1, keepdims=True)
            powers = jnp.where(allowed, jnp.exp(masked - highest), 0.0)
            shares = (powers / jnp.sum(powers, axis=-1, keepdims=True)).astype(jnp.bfloat16)
            result = jnp.dot(shares, value_rows, preferred_element_type=jnp.float32)
            mixed = result if head == 0 else jnp.where(here, result, mixed)
        attended[:, lanes] = mixed.astype(jnp.bfloat16)

    def out_copy(i, other, side):
        rows = pl.ds(row(offsets[i], other), 32)
        return pltpu.make_async_copy(
            partial.at[rows, halves[side]], outs[2 * i + other].at[:, halves[side]], out_sems.at[side, 2 * i + other]
        )

    out_copies = [[out_copy(i, other, side) for i in range(8) for other in range(2)] for side in range(2)]
    for k in range(chunks):
        weight_copy(3, k).wait()
        columns = pl.ds(k * chunk, chunk)
        partial[:, columns] = lax.dot_general(
            attended[...], held[3, columns, :], (((1,), (1,)), ((), ())), preferred_element_type=jnp.float32
        ).astype(jnp.bfloat16)
        if (k + 1) % (chunks // 2) == 0:
            for copy in out_copies[k // (chunks // 2)]:
                copy.start()
    for copy in out_copies[0] + out_copies[1]:
        copy.wait()


def layer(place, pairs, memories, weight, query_segs, key_segs):
    width = pairs[0].shape[1]
    tokens = query_segs.shape[0]
    anywhere = pl.BlockSpec(memory_space=pl.ANY)
    inside = pl.BlockSpec(memory_space=pltpu.VMEM)
    return pl.pallas_call(
        layer_kernel,
        out_shape=[jax.ShapeDtypeStruct((32, width), jnp.bfloat16)] * 16,
        in_specs=[pl.BlockSpec(memory_space=pltpu.SMEM)] + [anywhere] * 23 + [inside] * 2,
        out_specs=[anywhere] * 16,
        scratch_shapes=[
            pltpu.VMEM((2, tokens, width), jnp.bfloat16),
            pltpu.VMEM(weight.shape, jnp.bfloat16),
            pltpu.VMEM((3, tokens, weight.shape[2]), jnp.float32),
            pltpu.VMEM((tokens, weight.shape[2]), jnp.bfloat16),
            pltpu.VMEM((tokens, width), jnp.bfloat16),
            pltpu.SemaphoreType.DMA((2, 16)),
            pltpu.SemaphoreType.DMA((2, 4)),
            pltpu.SemaphoreType.DMA((4, 4)),
            pltpu.SemaphoreType.DMA((2, 16)),
        ],
        compiler_params=pltpu.CompilerParams(vmem_limit_bytes=60 * 1024 * 1024),
        cost_estimate=pl.CostEstimate(flops=7_000_000_000, bytes_accessed=20_000_000, transcendentals=1_000_000),
    )(place, *pairs, *memories, weight, query_segs, key_segs)


def gradient_kernel(logits, log_total, wanted, first, second, out, rows, slopes, sems):
    vocab, half = slopes.shape[1:]
    copies = [pltpu.make_async_copy(a, rows.at[i], sems.at[i]) for i, a in enumerate((first, second))]
    for copy in copies:
        copy.start()
    entry = lax.broadcasted_iota(jnp.int32, (vocab, half), 0)
    for i in range(2):
        owned = (entry == wanted[i : i + 1, :]).astype(jnp.float32)
        slopes[i] = (jnp.exp(logits[i] - log_total[i : i + 1, :]) - owned).astype(jnp.bfloat16)
    for copy in copies:
        copy.wait()
    chunk = 1024
    for k in range(out.shape[1] // chunk):
        columns = pl.ds(k * chunk, chunk)
        out[:, columns] = sum(
            jnp.dot(slopes[i], rows[i, :, columns], preferred_element_type=jnp.float32) for i in range(2)
        )


def gradient(logits, log_total, wanted, first, second):
    anywhere = pl.BlockSpec(memory_space=pl.ANY)
    inside = pl.BlockSpec(memory_space=pltpu.VMEM)
    return pl.pallas_call(
        gradient_kernel,
        out_shape=jax.ShapeDtypeStruct((logits.shape[1], first.shape[1]), jnp.float32),
        in_specs=[inside] * 3 + [anywhere] * 2,
        out_specs=inside,
        scratch_shapes=[
            pltpu.VMEM((2,) + first.shape, jnp.bfloat16),
            pltpu.VMEM(logits.shape, jnp.bfloat16),
            pltpu.SemaphoreType.DMA((2,)),
        ],
        compiler_params=pltpu.CompilerParams(vmem_limit_bytes=32 * 1024 * 1024),
        cost_estimate=pl.CostEstimate(flops=540_000_000, bytes_accessed=7_000_000, transcendentals=66_000),
    )(logits, log_total, wanted, first, second)


def spread_final(rows):
    half = rows.shape[0] // 2
    plane = lax.axis_index("y") * 2 + lax.axis_index("xh")
    moved = lax.ppermute(rows[:half], SECTION, [(15, 14)])
    mine = jnp.where(lax.axis_index("c") == 1, rows[half:], moved)
    moved = lax.ppermute(mine, ("y", "xh"), [(7, 6)])
    mine = jnp.where(plane == 6, moved, mine)
    first = lax.ppermute(mine, ("y", "xh"), [(7, 5), (6, 4)])
    second = lax.ppermute(mine, ("y", "xh"), [(7, 1), (6, 0)])
    third = lax.ppermute(mine, ("y", "xh"), [(7, 3), (6, 2)])
    return jnp.where(plane >= 6, mine, jnp.where(plane >= 4, first, jnp.where(plane < 2, second, third)))


def join(highest, total, picked):
    top = jnp.max(highest, axis=0)
    return jnp.stack([top, jnp.sum(total * jnp.exp(highest - top), axis=0), jnp.sum(picked, axis=0)])


def combine(stats, axis):
    count = lax.axis_size(axis)
    every = lax.all_to_all(jnp.broadcast_to(stats[None], (count,) + stats.shape), axis, 0, 0)
    return join(every[:, 0], every[:, 1], every[:, 2])


def per_device(
    states, section_segs, weights, gains, memory, memory_segs, final_gain, embedding, targets
):
    section_index = lax.axis_index(SECTION)
    core = lax.axis_index("c")
    z = lax.axis_index("z")
    column = lax.axis_index("xl")
    sign = 1 - 2 * (z % 2)
    current = states[0]
    normed = norm_rows(current, gains[0]).astype(jnp.bfloat16)

    rows = jnp.concatenate([memory, shift(memory, "xh", 1)], axis=0)
    rows = [rows] + [shift(rows, "y", d) for d in (1, 2, 3)]

    def swap_near(step, known, blocks):
        if step < 3:
            return known
        near = memory_of(blocks[:5])
        return near, shift(near, "c", 1)

    found, (near, near_swapped) = gather_blocks(jnp.concatenate([normed] + rows, axis=0), swap_near)
    pairs = [block for pair in found for block in pair]
    far = memory_of(found[5:])
    memories = [near, near_swapped, far, shift(far, "c", 1)]
    query_segs = jnp.swapaxes(section_segs[0].reshape(2, 8, 32), 0, 1).reshape(-1)
    decoding = (section_index >= 8).astype(jnp.int32)
    key_segs = jnp.where(decoding == 1, pick(memory_segs, memory_rows()), query_segs)
    place = jnp.stack([z, sign, column, decoding]).astype(jnp.int32)
    parts = layer(place, pairs, memories, weights[0], query_segs[:, None], key_segs[None, :])
    summed = scatter_blocks(parts[0::2], parts[1::2])
    updated = (current.astype(jnp.float32) + summed).astype(jnp.bfloat16)
    spread = spread_final(norm_rows(updated, final_gain).astype(jnp.bfloat16))
    forward = [(i, i + 1) for i in range(15) if i != 7]
    gathered, (next_states,) = gather_blocks(
        spread, lambda step, known, blocks: (lax.ppermute(updated[None], SECTION, forward),) if step == 1 else known
    )

    offsets = [0, sign, -sign, 2 * sign, -2 * sign, 3 * sign, -3 * sign, 4]
    far = [jnp.concatenate([gathered[7][i], gathered[8][i]], axis=1) for i in range(2)]
    rows = jnp.zeros((8, 2) + spread.shape, spread.dtype)
    for offset, pair in zip(offsets, gathered[:7] + [far]):
        for i in range(2):
            rows = lax.dynamic_update_slice(
                rows, pair[i][None, None], ((z + 8 + offset) % 8, column if i == 0 else 1 - column, 0, 0)
            )
    held = rows.reshape(256, -1)
    halves = [held, shift(held, "c", 1)]

    def flip(value):
        return jnp.where(core == 1, value[..., ::-1, :], value)

    at = jnp.arange(512, dtype=jnp.int32)
    tokens = (at // 16 % 2) * 256 + (at // 32 % 8) * 32 + (core ^ (at // 256)) * 16 + at % 16
    vocab_local = embedding.shape[0]
    vocab_start = (section_index * 16 + lax.axis_index(MP)) * vocab_local
    wanted = (pick(targets, tokens) - vocab_start).reshape(2, 256)
    logits = jnp.stack(
        [
            lax.dot_general(embedding, half, (((1,), (1,)), ((), ())), preferred_element_type=jnp.float32)
            for half in halves
        ]
    )
    owned = wanted[:, None, :] == jnp.arange(vocab_local, dtype=jnp.int32)[None, :, None]
    local_max = jnp.max(logits, axis=1)
    local_sum = jnp.sum(jnp.exp(logits - local_max[:, None]), axis=1)
    picked = jnp.sum(jnp.where(owned, logits, 0.0), axis=1)
    stats = flip(jnp.stack([local_max, local_sum, picked]))
    stats = combine(combine(stats, MP), SECTION)
    log_total = stats[0] + jnp.log(stats[1])
    loss = (log_total - stats[2]).reshape(2, 8, 2, 16).transpose(2, 1, 0, 3).reshape(-1)
    embed_grad = gradient(logits, flip(log_total), wanted, *halves)
    return (next_states, loss, embed_grad)


def solution(mesh):
    fine = Mesh(mesh.devices.reshape(4, 2, 2, 2, 8), ("y", "xh", "c", "xl", "z"))
    everything = P(SECTION + MP, None)
    placed = (
        P(SECTION, MP, None),
        P(SECTION, None),
        P(SECTION, None, None, MP),
        P(SECTION, None),
        everything,
        P(),
        P(),
        everything,
        P(),
    )
    return jax.shard_map(
        per_device,
        mesh=fine,
        in_specs=placed,
        out_specs=(P(SECTION, MP, None), P(), everything),
        check_vma=False,
    )
```

```python
import functools

import jax
import jax.numpy as jnp
from jax import lax
from jax.experimental import pallas as pl
from jax.experimental.pallas import tpu as pltpu
from jax.sharding import Mesh
from jax.sharding import PartitionSpec as P

HEAD_DIM = 64
SECTION = ("y", "xh", "c")
MP = ("xl", "z")


def shift(block, axis, distance):
    count = lax.axis_size(axis)
    return lax.ppermute(block, axis, [(i, (i + distance) % count) for i in range(count)])


def norm_rows(rows, gain_row):
    as_float = rows.astype(jnp.float32)
    inverse = lax.rsqrt(jnp.mean(as_float * as_float, axis=-1, keepdims=True) + 1e-06)
    return as_float * inverse * gain_row


together = lax.optimization_barrier


def inner(block):
    return lax.ppermute(block, "z", [(i, i ^ 1) for i in range(8)])


def outer(block):
    return lax.ppermute(block, "z", [(i, (i + 1) % 8 if i % 2 else (i - 1) % 8) for i in range(8)])


def across(block):
    return shift(block, "xl", 1)


def gather_blocks(block, crossing, in_step, beside=lambda step, known, blocks: known):
    half = block.shape[1] // 2
    own, other, fresh = [block], [], [block]
    ahead, behind = block, block
    side, pending = (), ()
    for step in range(4):
        if step < 3:
            behind, ahead = outer(ahead), inner(behind)
            arrived = (ahead, behind)
        else:
            arrived = (inner(behind[:, :half]), outer(ahead[:, half:]))
        crossed = tuple(across(b[:crossing]) for b in fresh)
        if in_step:
            pending = crossed
        side = beside(step, side, list(zip(own, other + list(pending))))
        arrived, pending, side = together((arrived, pending, side))
        if step < 3:
            ahead, behind = arrived
        own += arrived
        other += pending
        pending, fresh = () if in_step else crossed, arrived
    other += pending
    last = tuple(b[:crossing] for b in fresh)
    last, own = together((last, own))
    other += [across(b) for b in last]
    return list(zip(own, other)), side


def scatter_blocks(own, other):
    half = own[0].shape[1] // 2
    as_float = lambda a: a.astype(jnp.float32)
    narrow = lambda a: a.astype(jnp.bfloat16)
    other = list(other)
    far = narrow(as_float(own[7]) + as_float(across(other[7])))
    pending = (across(other[6]), across(other[5]))
    far, other[4], other[3] = together((far, other[4], other[3]))
    moved = (inner(far[:, :half]), outer(far[:, half:]))
    crossed = (across(other[4]), across(other[3]))
    (left, right), (one, two), other[2], other[1] = together((moved, pending, other[2], other[1]))
    minus = as_float(own[6]) + as_float(one)
    plus = as_float(own[5]) + as_float(two)
    up = narrow(jnp.concatenate([minus[:, :half] + as_float(left), minus[:, half:]], axis=1))
    down = narrow(jnp.concatenate([plus[:, :half], plus[:, half:] + as_float(right)], axis=1))
    for step in (2, 1):
        moved, pending = (outer(up), inner(down)), crossed
        if step == 2:
            crossed = (across(other[2]), across(other[1]))
        else:
            crossed = (across(other[0]),)
        (up, down), (one, two), other[0] = together((moved, pending, other[0]))
        up, down = (
            narrow(as_float(own[2 * step]) + as_float(one) + as_float(down)),
            narrow(as_float(own[2 * step - 1]) + as_float(two) + as_float(up)),
        )
    up, down = outer(up), inner(down)
    return as_float(own[0]) + as_float(crossed[0]) + as_float(up) + as_float(down)


def pick(values, index):
    places = jnp.arange(values.shape[0], dtype=jnp.int32)
    return jnp.sum(jnp.where(index[:, None] == places[None, :], values[None, :], 0), axis=1)


def memory_rows():
    at = jnp.arange(512, dtype=jnp.int32)
    core = lax.axis_index("c") ^ (at // 256)
    place = at % 256 // 32
    z = lax.axis_index("z")
    ahead = jnp.where(place % 2 == 1, (place + 1) // 2, -(place // 2)) * (1 - 2 * (z % 2))
    z = (z + 8 + ahead) % 8
    y = (lax.axis_index("y") + 4 - at // 8 % 4) % 4
    xh = lax.axis_index("xh") ^ (at // 4 % 2)
    column = lax.axis_index("xl") ^ (at // 2 % 2)
    return (y * 4 + xh * 2 + core) * 32 + (column * 8 + z) * 2 + at % 2


def memory_kernel(places, *refs):
    count = len(places)
    blocks, out, held, in_sems, out_sem = refs[:count], *refs[count:]
    copies = []
    for i, (row, column, width) in enumerate(places):
        target = held.at[pl.ds(row, 32), pl.ds(column, width)]
        copies.append(pltpu.make_async_copy(blocks[i].at[32:], target, in_sems.at[i]))
    for copy in copies:
        copy.start()
    for copy in copies:
        copy.wait()
    copy = pltpu.make_async_copy(held, out, out_sem)
    copy.start()
    copy.wait()


def memory_of(blocks):
    width = blocks[0].shape[1]
    whole = sum(block.shape[1] == width for block in blocks)
    rows = 32 * (whole + (len(blocks) - whole) // 2)
    places = [(32 * min(i, whole), max(i - whole, 0) * width // 2, b.shape[1]) for i, b in enumerate(blocks)]
    anywhere = pl.BlockSpec(memory_space=pl.ANY)
    return pl.pallas_call(
        functools.partial(memory_kernel, places),
        out_shape=jax.ShapeDtypeStruct((rows, width), blocks[0].dtype),
        in_specs=[anywhere] * len(blocks),
        out_specs=anywhere,
        scratch_shapes=[
            pltpu.VMEM((rows, width), blocks[0].dtype),
            pltpu.SemaphoreType.DMA((len(blocks),)),
            pltpu.SemaphoreType.DMA,
        ],
        compiler_params=pltpu.CompilerParams(vmem_limit_bytes=60 * 1024 * 1024),
        cost_estimate=pl.CostEstimate(flops=0, bytes_accessed=4_000_000, transcendentals=0),
    )(*blocks)


def layer_kernel(*refs):
    place = refs[0]
    pairs = refs[1:19]
    memory_refs = refs[19:21]
    weight, query_segs, key_segs = refs[21:24]
    outs = refs[24:40]
    source, held, total, attended, partial, in_sems, memory_sems, weight_sems, out_sems = refs[40:]
    z, sign, column, decoding = place[0], place[1], place[2], place[3]
    half = source.shape[2] // 2
    tokens, width = attended.shape
    chunk = 1024
    chunks = held.shape[1] // chunk
    halves = [pl.ds(0, half), pl.ds(half, half)]

    def row(offset, other):
        col = column if other == 0 else 1 - column
        return pl.multiple_of((lax.rem(z + 8 + offset, 8) * 2 + col) * 32, 32)

    offsets = [0, sign, -sign, 2 * sign, -2 * sign, 3 * sign, -3 * sign, 4]

    def pair_copy(i, other, side):
        rows = pl.ds(row(offsets[i], other), 32)
        block = pairs[2 * (i + side) + other].at[:32] if i == 7 else pairs[2 * i + other].at[:32, halves[side]]
        return pltpu.make_async_copy(block, source.at[0, rows, halves[side]], in_sems.at[side, 2 * i + other])

    def weight_copy(j, k):
        rows = pl.ds(k * chunk, chunk)
        return pltpu.make_async_copy(weight.at[j, rows], held.at[j, rows], weight_sems.at[j, k])

    def memory_copy(i, side):
        count = memory_refs[i].shape[0]
        first = sum(memory_refs[before].shape[0] for before in range(i))
        return pltpu.make_async_copy(
            memory_refs[i].at[:, halves[side]], source.at[1, pl.ds(first, count), halves[side]], memory_sems.at[side, i]
        )

    pair_copies = [[pair_copy(i, other, side) for i in range(8) for other in range(2)] for side in range(2)]
    memory_copies = [[memory_copy(i, side) for i in range(2)] for side in range(2)]
    for side in range(2):
        for copy in pair_copies[side]:
            copy.start()

        @pl.when(decoding == 1)
        def _():
            for copy in memory_copies[side]:
                copy.start()

        for k in range(side * chunks // 2, (side + 1) * chunks // 2):
            for j in range(3):
                weight_copy(j, k).start()
    for k in range(chunks):
        weight_copy(3, k).start()

    for k in range(chunks):
        if k % (chunks // 2) == 0:
            side = k // (chunks // 2)
            for copy in pair_copies[side]:
                copy.wait()

            @pl.when(decoding == 1)
            def _():
                for copy in memory_copies[side]:
                    copy.wait()

        for j in range(3):
            weight_copy(j, k).wait()
        columns = pl.ds(k * chunk, chunk)
        for j in range(3):
            rows = source[0, :, columns] if j == 0 else source[decoding, :, columns]
            part = jnp.dot(rows, held[j, columns, :], preferred_element_type=jnp.float32)
            if k == 0:
                total[j] = part
            else:
                total[j] += part

    allowed = query_segs[...] == key_segs[...]
    lane = lax.broadcasted_iota(jnp.int32, (1, 2 * HEAD_DIM), 1)
    for two in range(width // (2 * HEAD_DIM)):
        lanes = pl.ds(two * 2 * HEAD_DIM, 2 * HEAD_DIM)
        queries = total[0, :, lanes].astype(jnp.bfloat16)
        key_rows = total[1, :, lanes].astype(jnp.bfloat16)
        value_rows = total[2, :, lanes].astype(jnp.bfloat16)
        mixed = None
        for head in range(2):
            here = (lane // HEAD_DIM) == head
            one = jnp.where(here, queries, jnp.zeros_like(queries))
            scores = lax.dot_general(
                one, key_rows, (((1,), (1,)), ((), ())), preferred_element_type=jnp.float32
            )
            masked = jnp.where(allowed, scores, -1e30)
            highest = jnp.max(masked, axis=-1, keepdims=True)
            powers = jnp.where(allowed, jnp.exp(masked - highest), 0.0)
            shares = (powers / jnp.sum(powers, axis=-1, keepdims=True)).astype(jnp.bfloat16)
            result = jnp.dot(shares, value_rows, preferred_element_type=jnp.float32)
            mixed = result if head == 0 else jnp.where(here, result, mixed)
        attended[:, lanes] = mixed.astype(jnp.bfloat16)

    def out_copy(i, other, side):
        rows = pl.ds(row(offsets[i], other), 32)
        return pltpu.make_async_copy(
            partial.at[rows, halves[side]], outs[2 * i + other].at[:, halves[side]], out_sems.at[side, 2 * i + other]
        )

    out_copies = [[out_copy(i, other, side) for i in range(8) for other in range(2)] for side in range(2)]
    for k in range(chunks):
        weight_copy(3, k).wait()
        columns = pl.ds(k * chunk, chunk)
        partial[:, columns] = lax.dot_general(
            attended[...], held[3, columns, :], (((1,), (1,)), ((), ())), preferred_element_type=jnp.float32
        ).astype(jnp.bfloat16)
        if (k + 1) % (chunks // 2) == 0:
            for copy in out_copies[k // (chunks // 2)]:
                copy.start()
    for copy in out_copies[0] + out_copies[1]:
        copy.wait()


def layer(place, pairs, memories, weight, query_segs, key_segs):
    width = pairs[0].shape[1]
    tokens = query_segs.shape[0]
    anywhere = pl.BlockSpec(memory_space=pl.ANY)
    inside = pl.BlockSpec(memory_space=pltpu.VMEM)
    return pl.pallas_call(
        layer_kernel,
        out_shape=[jax.ShapeDtypeStruct((32, width), jnp.bfloat16)] * 16,
        in_specs=[pl.BlockSpec(memory_space=pltpu.SMEM)] + [anywhere] * 21 + [inside] * 2,
        out_specs=[anywhere] * 16,
        scratch_shapes=[
            pltpu.VMEM((2, tokens, width), jnp.bfloat16),
            pltpu.VMEM(weight.shape, jnp.bfloat16),
            pltpu.VMEM((3, tokens, weight.shape[2]), jnp.float32),
            pltpu.VMEM((tokens, weight.shape[2]), jnp.bfloat16),
            pltpu.VMEM((tokens, width), jnp.bfloat16),
            pltpu.SemaphoreType.DMA((2, 16)),
            pltpu.SemaphoreType.DMA((2, 2)),
            pltpu.SemaphoreType.DMA((4, 4)),
            pltpu.SemaphoreType.DMA((2, 16)),
        ],
        compiler_params=pltpu.CompilerParams(vmem_limit_bytes=60 * 1024 * 1024),
        cost_estimate=pl.CostEstimate(flops=7_000_000_000, bytes_accessed=20_000_000, transcendentals=1_000_000),
    )(place, *pairs, *memories, weight, query_segs, key_segs)


def gradient_kernel(logits, log_total, wanted, first, second, out, rows, slopes, sems):
    vocab, half = slopes.shape[1:]
    copies = [pltpu.make_async_copy(a, rows.at[i], sems.at[i]) for i, a in enumerate((first, second))]
    for copy in copies:
        copy.start()
    entry = lax.broadcasted_iota(jnp.int32, (vocab, half), 0)
    for i in range(2):
        owned = (entry == wanted[i : i + 1, :]).astype(jnp.float32)
        slopes[i] = (jnp.exp(logits[i] - log_total[i : i + 1, :]) - owned).astype(jnp.bfloat16)
    for copy in copies:
        copy.wait()
    chunk = 1024
    for k in range(out.shape[1] // chunk):
        columns = pl.ds(k * chunk, chunk)
        out[:, columns] = sum(
            jnp.dot(slopes[i], rows[i, :, columns], preferred_element_type=jnp.float32) for i in range(2)
        )


def gradient(logits, log_total, wanted, first, second):
    anywhere = pl.BlockSpec(memory_space=pl.ANY)
    inside = pl.BlockSpec(memory_space=pltpu.VMEM)
    return pl.pallas_call(
        gradient_kernel,
        out_shape=jax.ShapeDtypeStruct((logits.shape[1], first.shape[1]), jnp.float32),
        in_specs=[inside] * 3 + [anywhere] * 2,
        out_specs=inside,
        scratch_shapes=[
            pltpu.VMEM((2,) + first.shape, jnp.bfloat16),
            pltpu.VMEM(logits.shape, jnp.bfloat16),
            pltpu.SemaphoreType.DMA((2,)),
        ],
        compiler_params=pltpu.CompilerParams(vmem_limit_bytes=32 * 1024 * 1024),
        cost_estimate=pl.CostEstimate(flops=540_000_000, bytes_accessed=7_000_000, transcendentals=66_000),
    )(logits, log_total, wanted, first, second)


def spread_final(rows):
    half = rows.shape[0] // 2
    plane = lax.axis_index("y") * 2 + lax.axis_index("xh")
    top, bottom = rows[:half], rows[half:]
    here = lax.ppermute(top, SECTION, [(15, 14)])
    moved = [lax.ppermute(top, SECTION, [(15, 12)]), lax.ppermute(bottom, SECTION, [(15, 13)])]
    last = lax.axis_index("c") == 1
    mine = jnp.where(plane == 6, jnp.where(last, moved[1], moved[0]), jnp.where(last, bottom, here))
    first = lax.ppermute(mine, ("y", "xh"), [(7, 5), (6, 4)])
    second = lax.ppermute(mine, ("y", "xh"), [(7, 1), (6, 0)])
    third = lax.ppermute(mine, ("y", "xh"), [(7, 3), (6, 2)])
    return jnp.where(plane >= 6, mine, jnp.where(plane >= 4, first, jnp.where(plane < 2, second, third)))


def join(highest, total, picked):
    top = jnp.max(highest, axis=0)
    return jnp.stack([top, jnp.sum(total * jnp.exp(highest - top), axis=0), jnp.sum(picked, axis=0)])


def combine(stats, axis):
    count = lax.axis_size(axis)
    every = lax.all_to_all(jnp.broadcast_to(stats[None], (count,) + stats.shape), axis, 0, 0)
    return join(every[:, 0], every[:, 1], every[:, 2])


def per_device(
    states, section_segs, weights, gains, memory, memory_segs, final_gain, embedding, targets
):
    section_index = lax.axis_index(SECTION)
    core = lax.axis_index("c")
    z = lax.axis_index("z")
    column = lax.axis_index("xl")
    sign = 1 - 2 * (z % 2)
    current = states[0]
    normed = norm_rows(current, gains[0]).astype(jnp.bfloat16)

    moves = [(0, 1), (1, 0), (1, 1)]
    routes = [[(i, i ^ (2 * a + b)) for i in range(4)] for a, b in moves]
    rows = jnp.concatenate([memory] + [lax.ppermute(memory, ("xh", "xl"), route) for route in routes], axis=0)
    rows = [rows] + [shift(rows, "y", d) for d in (1, 2, 3)]

    found, _ = gather_blocks(jnp.concatenate([normed] + rows, axis=0), 32, True)
    pairs = [block for pair in found for block in pair]
    mine = memory_of(pairs[::2])
    memories = [mine, shift(mine, "c", 1)]
    query_segs = jnp.swapaxes(section_segs[0].reshape(2, 8, 32), 0, 1).reshape(-1)
    decoding = (section_index >= 8).astype(jnp.int32)
    key_segs = jnp.where(decoding == 1, pick(memory_segs, memory_rows()), query_segs)
    place = jnp.stack([z, sign, column, decoding]).astype(jnp.int32)
    parts = layer(place, pairs, memories, weights[0], query_segs[:, None], key_segs[None, :])
    summed = scatter_blocks(parts[0::2], parts[1::2])
    updated = (current.astype(jnp.float32) + summed).astype(jnp.bfloat16)
    spread = spread_final(norm_rows(updated, final_gain).astype(jnp.bfloat16))
    forward = [(i, i + 1) for i in range(15) if i != 7]
    gathered, (next_states,) = gather_blocks(
        spread, 16, False, lambda step, known, blocks: (lax.ppermute(updated[None], SECTION, forward),) if step == 1 else known
    )

    offsets = [0, sign, -sign, 2 * sign, -2 * sign, 3 * sign, -3 * sign, 4]
    far = [jnp.concatenate([gathered[7][i], gathered[8][i]], axis=1) for i in range(2)]
    rows = jnp.zeros((8, 2) + spread.shape, spread.dtype)
    for offset, pair in zip(offsets, gathered[:7] + [far]):
        for i in range(2):
            rows = lax.dynamic_update_slice(
                rows, pair[i][None, None], ((z + 8 + offset) % 8, column if i == 0 else 1 - column, 0, 0)
            )
    held = rows.reshape(256, -1)
    halves = [held, shift(held, "c", 1)]

    def flip(value):
        return jnp.where(core == 1, value[..., ::-1, :], value)

    at = jnp.arange(512, dtype=jnp.int32)
    tokens = (at // 16 % 2) * 256 + (at // 32 % 8) * 32 + (core ^ (at // 256)) * 16 + at % 16
    vocab_local = embedding.shape[0]
    vocab_start = (section_index * 16 + lax.axis_index(MP)) * vocab_local
    wanted = (pick(targets, tokens) - vocab_start).reshape(2, 256)
    logits = jnp.stack(
        [
            lax.dot_general(embedding, half, (((1,), (1,)), ((), ())), preferred_element_type=jnp.float32)
            for half in halves
        ]
    )
    owned = wanted[:, None, :] == jnp.arange(vocab_local, dtype=jnp.int32)[None, :, None]
    local_max = jnp.max(logits, axis=1)
    local_sum = jnp.sum(jnp.exp(logits - local_max[:, None]), axis=1)
    picked = jnp.sum(jnp.where(owned, logits, 0.0), axis=1)
    stats = flip(jnp.stack([local_max, local_sum, picked]))
    stats = combine(combine(stats, MP), SECTION)
    log_total = stats[0] + jnp.log(stats[1])
    loss = (log_total - stats[2]).reshape(2, 8, 2, 16).transpose(2, 1, 0, 3).reshape(-1)
    embed_grad = gradient(logits, flip(log_total), wanted, *halves)
    return (next_states, loss, embed_grad)


def solution(mesh):
    fine = Mesh(mesh.devices.reshape(4, 2, 2, 2, 8), ("y", "xh", "c", "xl", "z"))
    everything = P(SECTION + MP, None)
    placed = (
        P(SECTION, MP, None),
        P(SECTION, None),
        P(SECTION, None, None, MP),
        P(SECTION, None),
        everything,
        P(),
        P(),
        everything,
        P(),
    )
    return jax.shard_map(
        per_device,
        mesh=fine,
        in_specs=placed,
        out_specs=(P(SECTION, MP, None), P(), everything),
        check_vma=False,
    )
```

```python
import functools

import jax
import jax.numpy as jnp
from jax import lax
from jax.experimental import pallas as pl
from jax.experimental.pallas import tpu as pltpu
from jax.sharding import Mesh
from jax.sharding import PartitionSpec as P

HEAD_DIM = 64
SECTION = ("y", "xh", "c")
MP = ("xl", "z")


def shift(block, axis, distance):
    count = lax.axis_size(axis)
    return lax.ppermute(block, axis, [(i, (i + distance) % count) for i in range(count)])


def norm_rows(rows, gain_row):
    as_float = rows.astype(jnp.float32)
    inverse = lax.rsqrt(jnp.mean(as_float * as_float, axis=-1, keepdims=True) + 1e-06)
    return as_float * inverse * gain_row


together = lax.optimization_barrier


def inner(block):
    return lax.ppermute(block, "z", [(i, i ^ 1) for i in range(8)])


def outer(block):
    return lax.ppermute(block, "z", [(i, (i + 1) % 8 if i % 2 else (i - 1) % 8) for i in range(8)])


def across(block):
    return shift(block, "xl", 1)


def gather_blocks(block, beside):
    half = block.shape[1] // 2
    own, other, fresh = [block], [], [block]
    ahead, behind = block, block
    side, pending = (), ()
    for step in range(4):
        if step < 3:
            behind, ahead = outer(ahead), inner(behind)
            arrived = (ahead, behind)
        else:
            arrived = (inner(behind[:, :half]), outer(ahead[:, half:]))
        crossed = tuple(across(b) for b in fresh)
        side = beside(step, side)
        arrived, pending, side = together((arrived, pending, side))
        if step < 3:
            ahead, behind = arrived
        own += arrived
        other += pending
        pending, fresh = crossed, arrived
    other += pending
    other += [across(b) for b in fresh]
    return list(zip(own, other)), side


def scatter_blocks(own, other):
    half = own[0].shape[1] // 2
    as_float = lambda a: a.astype(jnp.float32)
    narrow = lambda a: a.astype(jnp.bfloat16)
    other = list(other)
    far = narrow(as_float(own[7]) + as_float(across(other[7])))
    pending = (across(other[6]), across(other[5]))
    far, other[4], other[3] = together((far, other[4], other[3]))
    moved = (inner(far[:, :half]), outer(far[:, half:]))
    crossed = (across(other[4]), across(other[3]))
    (left, right), (one, two), other[2], other[1] = together((moved, pending, other[2], other[1]))
    minus = as_float(own[6]) + as_float(one)
    plus = as_float(own[5]) + as_float(two)
    up = narrow(jnp.concatenate([minus[:, :half] + as_float(left), minus[:, half:]], axis=1))
    down = narrow(jnp.concatenate([plus[:, :half], plus[:, half:] + as_float(right)], axis=1))
    for step in (2, 1):
        moved, pending = (outer(up), inner(down)), crossed
        if step == 2:
            crossed = (across(other[2]), across(other[1]))
        else:
            crossed = (across(other[0]),)
        (up, down), (one, two), other[0] = together((moved, pending, other[0]))
        up, down = (
            narrow(as_float(own[2 * step]) + as_float(one) + as_float(down)),
            narrow(as_float(own[2 * step - 1]) + as_float(two) + as_float(up)),
        )
    up, down = outer(up), inner(down)
    return as_float(own[0]) + as_float(crossed[0]) + as_float(up) + as_float(down)


def pick(values, index):
    places = jnp.arange(values.shape[0], dtype=jnp.int32)
    return jnp.sum(jnp.where(index[:, None] == places[None, :], values[None, :], 0), axis=1)


def memory_rows():
    at = jnp.arange(512, dtype=jnp.int32)
    core = lax.axis_index("c") ^ (at // 256)
    place = at % 256 // 32
    z = lax.axis_index("z")
    ahead = jnp.where(place % 2 == 1, (place + 1) // 2, -(place // 2)) * (1 - 2 * (z % 2))
    z = (z + 8 + ahead) % 8
    y = (lax.axis_index("y") + 4 - at // 8 % 4) % 4
    xh = lax.axis_index("xh") ^ (at // 4 % 2)
    column = lax.axis_index("xl") ^ (at // 2 % 2)
    return (y * 4 + xh * 2 + core) * 32 + (column * 8 + z) * 2 + at % 2


def join_kernel(*refs):
    count = len(refs) - 4
    blocks, out, held, in_sems, out_sem = refs[:count], *refs[count:]
    rows = blocks[0].shape[0]
    copies = [
        pltpu.make_async_copy(blocks[i], held.at[pl.ds(rows * i, rows)], in_sems.at[i]) for i in range(count)
    ]
    for copy in copies:
        copy.start()
    for copy in copies:
        copy.wait()
    copy = pltpu.make_async_copy(held, out, out_sem)
    copy.start()
    copy.wait()


def join_rows(blocks):
    shape = (len(blocks) * blocks[0].shape[0], blocks[0].shape[1])
    anywhere = pl.BlockSpec(memory_space=pl.ANY)
    return pl.pallas_call(
        join_kernel,
        out_shape=jax.ShapeDtypeStruct(shape, blocks[0].dtype),
        in_specs=[anywhere] * len(blocks),
        out_specs=anywhere,
        scratch_shapes=[
            pltpu.VMEM(shape, blocks[0].dtype),
            pltpu.SemaphoreType.DMA((len(blocks),)),
            pltpu.SemaphoreType.DMA,
        ],
        compiler_params=pltpu.CompilerParams(vmem_limit_bytes=60 * 1024 * 1024),
        cost_estimate=pl.CostEstimate(flops=0, bytes_accessed=4_000_000, transcendentals=0),
    )(*blocks)


def layer_kernel(*refs):
    place = refs[0]
    pairs = refs[1:19]
    memory_refs = refs[19:25]
    weight, query_segs, key_segs = refs[25:28]
    outs = refs[28:44]
    source, held, total, attended, partial, in_sems, memory_sems, weight_sems, out_sems = refs[44:]
    z, sign, column, decoding = place[0], place[1], place[2], place[3]
    half = source.shape[2] // 2
    tokens, width = attended.shape
    chunk = 1024
    chunks = held.shape[1] // chunk
    halves = [pl.ds(0, half), pl.ds(half, half)]

    def row(offset, other):
        col = column if other == 0 else 1 - column
        return pl.multiple_of((lax.rem(z + 8 + offset, 8) * 2 + col) * 32, 32)

    offsets = [0, sign, -sign, 2 * sign, -2 * sign, 3 * sign, -3 * sign, 4]

    def pair_copy(i, other, side):
        rows = pl.ds(row(offsets[i], other), 32)
        block = pairs[2 * (i + side) + other] if i == 7 else pairs[2 * i + other].at[:, halves[side]]
        return pltpu.make_async_copy(block, source.at[0, rows, halves[side]], in_sems.at[side, 2 * i + other])

    def weight_copy(j, k):
        rows = pl.ds(k * chunk, chunk)
        return pltpu.make_async_copy(weight.at[j, rows], held.at[j, rows], weight_sems.at[j, k])

    def memory_copy(i, side):
        near, left, right = memory_refs[3 * (i // 2) : 3 * (i // 2) + 3]
        count, first = near.shape[0], 256 * (i // 2)
        rows = pl.ds(first, count) if i % 2 == 0 else pl.ds(first + count, 256 - count)
        block = near.at[:, halves[side]] if i % 2 == 0 else (left, right)[side]
        return pltpu.make_async_copy(block, source.at[1, rows, halves[side]], memory_sems.at[side, i])

    pair_copies = [[pair_copy(i, other, side) for i in range(8) for other in range(2)] for side in range(2)]
    memory_copies = [[memory_copy(i, side) for i in range(4)] for side in range(2)]
    for side in range(2):
        for copy in pair_copies[side]:
            copy.start()

        @pl.when(decoding == 1)
        def _():
            for copy in memory_copies[side]:
                copy.start()

        for k in range(side * chunks // 2, (side + 1) * chunks // 2):
            for j in range(3):
                weight_copy(j, k).start()
    for k in range(chunks):
        weight_copy(3, k).start()

    for k in range(chunks):
        if k % (chunks // 2) == 0:
            side = k // (chunks // 2)
            for copy in pair_copies[side]:
                copy.wait()

            @pl.when(decoding == 1)
            def _():
                for copy in memory_copies[side]:
                    copy.wait()

        for j in range(3):
            weight_copy(j, k).wait()
        columns = pl.ds(k * chunk, chunk)
        for j in range(3):
            rows = source[0, :, columns] if j == 0 else source[decoding, :, columns]
            part = jnp.dot(rows, held[j, columns, :], preferred_element_type=jnp.float32)
            if k == 0:
                total[j] = part
            else:
                total[j] += part

    allowed = query_segs[...] == key_segs[...]
    lane = lax.broadcasted_iota(jnp.int32, (1, 2 * HEAD_DIM), 1)
    for two in range(width // (2 * HEAD_DIM)):
        lanes = pl.ds(two * 2 * HEAD_DIM, 2 * HEAD_DIM)
        queries = total[0, :, lanes].astype(jnp.bfloat16)
        key_rows = total[1, :, lanes].astype(jnp.bfloat16)
        value_rows = total[2, :, lanes].astype(jnp.bfloat16)
        mixed = None
        for head in range(2):
            here = (lane // HEAD_DIM) == head
            one = jnp.where(here, queries, jnp.zeros_like(queries))
            scores = lax.dot_general(
                one, key_rows, (((1,), (1,)), ((), ())), preferred_element_type=jnp.float32
            )
            masked = jnp.where(allowed, scores, -1e30)
            highest = jnp.max(masked, axis=-1, keepdims=True)
            powers = jnp.where(allowed, jnp.exp(masked - highest), 0.0)
            shares = (powers / jnp.sum(powers, axis=-1, keepdims=True)).astype(jnp.bfloat16)
            result = jnp.dot(shares, value_rows, preferred_element_type=jnp.float32)
            mixed = result if head == 0 else jnp.where(here, result, mixed)
        attended[:, lanes] = mixed.astype(jnp.bfloat16)

    def out_copy(i, other, side):
        rows = pl.ds(row(offsets[i], other), 32)
        return pltpu.make_async_copy(
            partial.at[rows, halves[side]], outs[2 * i + other].at[:, halves[side]], out_sems.at[side, 2 * i + other]
        )

    out_copies = [[out_copy(i, other, side) for i in range(8) for other in range(2)] for side in range(2)]
    for k in range(chunks):
        weight_copy(3, k).wait()
        columns = pl.ds(k * chunk, chunk)
        partial[:, columns] = lax.dot_general(
            attended[...], held[3, columns, :], (((1,), (1,)), ((), ())), preferred_element_type=jnp.float32
        ).astype(jnp.bfloat16)
        if (k + 1) % (chunks // 2) == 0:
            for copy in out_copies[k // (chunks // 2)]:
                copy.start()
    for copy in out_copies[0] + out_copies[1]:
        copy.wait()


def layer(place, pairs, memories, weight, query_segs, key_segs):
    width = pairs[0].shape[1]
    tokens = query_segs.shape[0]
    anywhere = pl.BlockSpec(memory_space=pl.ANY)
    inside = pl.BlockSpec(memory_space=pltpu.VMEM)
    return pl.pallas_call(
        layer_kernel,
        out_shape=[jax.ShapeDtypeStruct((32, width), jnp.bfloat16)] * 16,
        in_specs=[pl.BlockSpec(memory_space=pltpu.SMEM)] + [anywhere] * 25 + [inside] * 2,
        out_specs=[anywhere] * 16,
        scratch_shapes=[
            pltpu.VMEM((2, tokens, width), jnp.bfloat16),
            pltpu.VMEM(weight.shape, jnp.bfloat16),
            pltpu.VMEM((3, tokens, weight.shape[2]), jnp.float32),
            pltpu.VMEM((tokens, weight.shape[2]), jnp.bfloat16),
            pltpu.VMEM((tokens, width), jnp.bfloat16),
            pltpu.SemaphoreType.DMA((2, 16)),
            pltpu.SemaphoreType.DMA((2, 4)),
            pltpu.SemaphoreType.DMA((4, 4)),
            pltpu.SemaphoreType.DMA((2, 16)),
        ],
        compiler_params=pltpu.CompilerParams(vmem_limit_bytes=60 * 1024 * 1024),
        cost_estimate=pl.CostEstimate(flops=7_000_000_000, bytes_accessed=20_000_000, transcendentals=1_000_000),
    )(place, *pairs, *memories, weight, query_segs, key_segs)


def gradient_kernel(logits, log_total, wanted, first, second, out, rows, slopes, sems):
    vocab, half = slopes.shape[1:]
    copies = [pltpu.make_async_copy(a, rows.at[i], sems.at[i]) for i, a in enumerate((first, second))]
    for copy in copies:
        copy.start()
    entry = lax.broadcasted_iota(jnp.int32, (vocab, half), 0)
    for i in range(2):
        owned = (entry == wanted[i : i + 1, :]).astype(jnp.float32)
        slopes[i] = (jnp.exp(logits[i] - log_total[i : i + 1, :]) - owned).astype(jnp.bfloat16)
    for copy in copies:
        copy.wait()
    chunk = 1024
    for k in range(out.shape[1] // chunk):
        columns = pl.ds(k * chunk, chunk)
        out[:, columns] = sum(
            jnp.dot(slopes[i], rows[i, :, columns], preferred_element_type=jnp.float32) for i in range(2)
        )


def gradient(logits, log_total, wanted, first, second):
    anywhere = pl.BlockSpec(memory_space=pl.ANY)
    inside = pl.BlockSpec(memory_space=pltpu.VMEM)
    return pl.pallas_call(
        gradient_kernel,
        out_shape=jax.ShapeDtypeStruct((logits.shape[1], first.shape[1]), jnp.float32),
        in_specs=[inside] * 3 + [anywhere] * 2,
        out_specs=inside,
        scratch_shapes=[
            pltpu.VMEM((2,) + first.shape, jnp.bfloat16),
            pltpu.VMEM(logits.shape, jnp.bfloat16),
            pltpu.SemaphoreType.DMA((2,)),
        ],
        compiler_params=pltpu.CompilerParams(vmem_limit_bytes=32 * 1024 * 1024),
        cost_estimate=pl.CostEstimate(flops=540_000_000, bytes_accessed=7_000_000, transcendentals=66_000),
    )(logits, log_total, wanted, first, second)


def spread_final(rows):
    half = rows.shape[0] // 2
    plane = lax.axis_index("y") * 2 + lax.axis_index("xh")
    top, bottom = rows[:half], rows[half:]
    here = lax.ppermute(top, SECTION, [(15, 14)])
    moved = [lax.ppermute(top, SECTION, [(15, 12)]), lax.ppermute(bottom, SECTION, [(15, 13)])]
    last = lax.axis_index("c") == 1
    mine = jnp.where(plane == 6, jnp.where(last, moved[1], moved[0]), jnp.where(last, bottom, here))
    first = lax.ppermute(mine, ("y", "xh"), [(7, 5), (6, 4)])
    second = lax.ppermute(mine, ("y", "xh"), [(7, 1), (6, 0)])
    third = lax.ppermute(mine, ("y", "xh"), [(7, 3), (6, 2)])
    return jnp.where(plane >= 6, mine, jnp.where(plane >= 4, first, jnp.where(plane < 2, second, third)))


def join(highest, total, picked):
    top = jnp.max(highest, axis=0)
    return jnp.stack([top, jnp.sum(total * jnp.exp(highest - top), axis=0), jnp.sum(picked, axis=0)])


def combine(stats, axis):
    count = lax.axis_size(axis)
    every = lax.all_to_all(jnp.broadcast_to(stats[None], (count,) + stats.shape), axis, 0, 0)
    return join(every[:, 0], every[:, 1], every[:, 2])


def per_device(
    states, section_segs, weights, gains, memory, memory_segs, final_gain, embedding, targets
):
    section_index = lax.axis_index(SECTION)
    core = lax.axis_index("c")
    z = lax.axis_index("z")
    column = lax.axis_index("xl")
    sign = 1 - 2 * (z % 2)
    current = states[0]
    normed = norm_rows(current, gains[0]).astype(jnp.bfloat16)

    moves = [(0, 1), (1, 0), (1, 1)]
    routes = [[(i, i ^ (2 * a + b)) for i in range(4)] for a, b in moves]

    def memory_ring(step, known):
        if step == 0:
            rows = jnp.concatenate([memory] + [lax.ppermute(memory, ("xh", "xl"), route) for route in routes], axis=0)
            return (jnp.concatenate([rows] + [shift(rows, "y", d) for d in (1, 2, 3)], axis=0),)
        ahead, behind = (known * 2)[:2] if step == 1 else known[-2:]
        return known + (inner(behind), outer(ahead))

    found, near = gather_blocks(normed, memory_ring)
    pairs = [block for pair in found for block in pair]
    half = normed.shape[1] // 2
    far = [inner(near[-1][:, :half]), outer(near[-2][:, half:])]
    mine = [join_rows(near)] + far
    memories = mine + [shift(block, "c", 1) for block in mine]
    query_segs = jnp.swapaxes(section_segs[0].reshape(2, 8, 32), 0, 1).reshape(-1)
    decoding = (section_index >= 8).astype(jnp.int32)
    key_segs = jnp.where(decoding == 1, pick(memory_segs, memory_rows()), query_segs)
    place = jnp.stack([z, sign, column, decoding]).astype(jnp.int32)
    parts = layer(place, pairs, memories, weights[0], query_segs[:, None], key_segs[None, :])
    summed = scatter_blocks(parts[0::2], parts[1::2])
    updated = (current.astype(jnp.float32) + summed).astype(jnp.bfloat16)
    spread = spread_final(norm_rows(updated, final_gain).astype(jnp.bfloat16))
    forward = [(i, i + 1) for i in range(15) if i != 7]
    gathered, (next_states,) = gather_blocks(
        spread, lambda step, known: (lax.ppermute(updated[None], SECTION, forward),) if step == 1 else known
    )

    offsets = [0, sign, -sign, 2 * sign, -2 * sign, 3 * sign, -3 * sign, 4]
    far = [jnp.concatenate([gathered[7][i], gathered[8][i]], axis=1) for i in range(2)]
    rows = jnp.zeros((8, 2) + spread.shape, spread.dtype)
    for offset, pair in zip(offsets, gathered[:7] + [far]):
        for i in range(2):
            rows = lax.dynamic_update_slice(
                rows, pair[i][None, None], ((z + 8 + offset) % 8, column if i == 0 else 1 - column, 0, 0)
            )
    held = rows.reshape(256, -1)
    halves = [held, shift(held, "c", 1)]

    def flip(value):
        return jnp.where(core == 1, value[..., ::-1, :], value)

    at = jnp.arange(512, dtype=jnp.int32)
    tokens = (at // 16 % 2) * 256 + (at // 32 % 8) * 32 + (core ^ (at // 256)) * 16 + at % 16
    vocab_local = embedding.shape[0]
    vocab_start = (section_index * 16 + lax.axis_index(MP)) * vocab_local
    wanted = (pick(targets, tokens) - vocab_start).reshape(2, 256)
    logits = jnp.stack(
        [
            lax.dot_general(embedding, half, (((1,), (1,)), ((), ())), preferred_element_type=jnp.float32)
            for half in halves
        ]
    )
    owned = wanted[:, None, :] == jnp.arange(vocab_local, dtype=jnp.int32)[None, :, None]
    local_max = jnp.max(logits, axis=1)
    local_sum = jnp.sum(jnp.exp(logits - local_max[:, None]), axis=1)
    picked = jnp.sum(jnp.where(owned, logits, 0.0), axis=1)
    stats = flip(jnp.stack([local_max, local_sum, picked]))
    stats = combine(combine(stats, MP), SECTION)
    log_total = stats[0] + jnp.log(stats[1])
    loss = (log_total - stats[2]).reshape(2, 8, 2, 16).transpose(2, 1, 0, 3).reshape(-1)
    embed_grad = gradient(logits, flip(log_total), wanted, *halves)
    return (next_states, loss, embed_grad)


def solution(mesh):
    fine = Mesh(mesh.devices.reshape(4, 2, 2, 2, 8), ("y", "xh", "c", "xl", "z"))
    everything = P(SECTION + MP, None)
    placed = (
        P(SECTION, MP, None),
        P(SECTION, None),
        P(SECTION, None, None, MP),
        P(SECTION, None),
        everything,
        P(),
        P(),
        everything,
        P(),
    )
    return jax.shard_map(
        per_device,
        mesh=fine,
        in_specs=placed,
        out_specs=(P(SECTION, MP, None), P(), everything),
        check_vma=False,
    )
```

```python
import functools

import jax
import jax.numpy as jnp
from jax import lax
from jax.experimental import pallas as pl
from jax.experimental.pallas import tpu as pltpu
from jax.sharding import Mesh
from jax.sharding import PartitionSpec as P

HEAD_DIM = 64
SECTION = ("y", "xh", "c")
MP = ("xl", "z")


def shift(block, axis, distance):
    count = lax.axis_size(axis)
    return lax.ppermute(block, axis, [(i, (i + distance) % count) for i in range(count)])


def norm_rows(rows, gain_row):
    as_float = rows.astype(jnp.float32)
    inverse = lax.rsqrt(jnp.mean(as_float * as_float, axis=-1, keepdims=True) + 1e-06)
    return as_float * inverse * gain_row


together = lax.optimization_barrier


def inner(block):
    return lax.ppermute(block, "z", [(i, i ^ 1) for i in range(8)])


def outer(block):
    return lax.ppermute(block, "z", [(i, (i + 1) % 8 if i % 2 else (i - 1) % 8) for i in range(8)])


def across(block):
    return shift(block, "xl", 1)


def gather_blocks(block, beside, settle=False):
    half = block.shape[1] // 2
    own, other, fresh = [block], [], [block]
    ahead, behind = block, block
    side, pending = (), ()
    for step in range(4):
        if step < 3:
            behind, ahead = outer(ahead), inner(behind)
            arrived = (ahead, behind)
        else:
            arrived = (inner(behind[:, :half]), outer(ahead[:, half:]))
        crossed = tuple(across(b) for b in fresh)
        side = beside(step, side)
        if settle and step == 3:
            arrived, pending, crossed, side = together((arrived, pending, crossed, side))
        else:
            arrived, pending, side = together((arrived, pending, side))
        if step < 3:
            ahead, behind = arrived
        own += arrived
        other += pending
        pending, fresh = crossed, arrived
    other += pending
    other += [across(b) for b in fresh]
    return list(zip(own, other)), side


def scatter_blocks(own, other):
    half = own[0].shape[1] // 2
    as_float = lambda a: a.astype(jnp.float32)
    narrow = lambda a: a.astype(jnp.bfloat16)
    other = list(other)
    far = narrow(as_float(own[7]) + as_float(across(other[7])))
    pending = (across(other[6]), across(other[5]))
    far, other[4], other[3] = together((far, other[4], other[3]))
    moved = (inner(far[:, :half]), outer(far[:, half:]))
    crossed = (across(other[4]), across(other[3]))
    (left, right), (one, two), other[2], other[1] = together((moved, pending, other[2], other[1]))
    minus = as_float(own[6]) + as_float(one)
    plus = as_float(own[5]) + as_float(two)
    up = narrow(jnp.concatenate([minus[:, :half] + as_float(left), minus[:, half:]], axis=1))
    down = narrow(jnp.concatenate([plus[:, :half], plus[:, half:] + as_float(right)], axis=1))
    for step in (2, 1):
        moved, pending = (outer(up), inner(down)), crossed
        if step == 2:
            crossed = (across(other[2]), across(other[1]))
        else:
            crossed = (across(other[0]),)
        (up, down), (one, two), other[0] = together((moved, pending, other[0]))
        up, down = (
            narrow(as_float(own[2 * step]) + as_float(one) + as_float(down)),
            narrow(as_float(own[2 * step - 1]) + as_float(two) + as_float(up)),
        )
    up, down = outer(up), inner(down)
    return as_float(own[0]) + as_float(crossed[0]) + as_float(up) + as_float(down)


def pick(values, index):
    places = jnp.arange(values.shape[0], dtype=jnp.int32)
    return jnp.sum(jnp.where(index[:, None] == places[None, :], values[None, :], 0), axis=1)


def memory_rows():
    at = jnp.arange(512, dtype=jnp.int32)
    core = lax.axis_index("c") ^ (at // 256)
    place = at % 256 // 32
    z = lax.axis_index("z")
    ahead = jnp.where(place % 2 == 1, (place + 1) // 2, -(place // 2)) * (1 - 2 * (z % 2))
    z = (z + 8 + ahead) % 8
    y = (lax.axis_index("y") + 4 - at // 8 % 4) % 4
    xh = lax.axis_index("xh") ^ (at // 4 % 2)
    column = lax.axis_index("xl") ^ (at // 2 % 2)
    return (y * 4 + xh * 2 + core) * 32 + (column * 8 + z) * 2 + at % 2


def join_kernel(*refs):
    count = len(refs) - 4
    blocks, out, held, in_sems, out_sem = refs[:count], *refs[count:]
    rows = blocks[0].shape[0]
    copies = [
        pltpu.make_async_copy(blocks[i], held.at[pl.ds(rows * i, rows)], in_sems.at[i]) for i in range(count)
    ]
    for copy in copies:
        copy.start()
    for copy in copies:
        copy.wait()
    copy = pltpu.make_async_copy(held, out, out_sem)
    copy.start()
    copy.wait()


def join_rows(blocks):
    shape = (len(blocks) * blocks[0].shape[0], blocks[0].shape[1])
    anywhere = pl.BlockSpec(memory_space=pl.ANY)
    return pl.pallas_call(
        join_kernel,
        out_shape=jax.ShapeDtypeStruct(shape, blocks[0].dtype),
        in_specs=[anywhere] * len(blocks),
        out_specs=anywhere,
        scratch_shapes=[
            pltpu.VMEM(shape, blocks[0].dtype),
            pltpu.SemaphoreType.DMA((len(blocks),)),
            pltpu.SemaphoreType.DMA,
        ],
        compiler_params=pltpu.CompilerParams(vmem_limit_bytes=60 * 1024 * 1024),
        cost_estimate=pl.CostEstimate(flops=0, bytes_accessed=4_000_000, transcendentals=0),
    )(*blocks)


def layer_kernel(*refs):
    place = refs[0]
    pairs = refs[1:19]
    memory_refs = refs[19:25]
    weight, query_segs, key_segs = refs[25:28]
    outs = refs[28:44]
    source, held, total, attended, partial, in_sems, memory_sems, weight_sems, out_sems = refs[44:]
    z, sign, column, decoding = place[0], place[1], place[2], place[3]
    half = source.shape[2] // 2
    tokens, width = attended.shape
    chunk = 1024
    chunks = held.shape[1] // chunk
    halves = [pl.ds(0, half), pl.ds(half, half)]

    def row(offset, other):
        col = column if other == 0 else 1 - column
        return pl.multiple_of((lax.rem(z + 8 + offset, 8) * 2 + col) * 32, 32)

    offsets = [0, sign, -sign, 2 * sign, -2 * sign, 3 * sign, -3 * sign, 4]

    def pair_copy(i, other, side):
        rows = pl.ds(row(offsets[i], other), 32)
        block = pairs[2 * (i + side) + other] if i == 7 else pairs[2 * i + other].at[:, halves[side]]
        return pltpu.make_async_copy(block, source.at[0, rows, halves[side]], in_sems.at[side, 2 * i + other])

    def weight_copy(j, k):
        rows = pl.ds(k * chunk, chunk)
        return pltpu.make_async_copy(weight.at[j, rows], held.at[j, rows], weight_sems.at[j, k])

    def memory_copy(i, side):
        near, left, right = memory_refs[3 * (i // 2) : 3 * (i // 2) + 3]
        count, first = near.shape[0], 256 * (i // 2)
        rows = pl.ds(first, count) if i % 2 == 0 else pl.ds(first + count, 256 - count)
        block = near.at[:, halves[side]] if i % 2 == 0 else (left, right)[side]
        return pltpu.make_async_copy(block, source.at[1, rows, halves[side]], memory_sems.at[side, i])

    pair_copies = [[pair_copy(i, other, side) for i in range(8) for other in range(2)] for side in range(2)]
    memory_copies = [[memory_copy(i, side) for i in range(4)] for side in range(2)]
    for side in range(2):
        for copy in pair_copies[side]:
            copy.start()

        @pl.when(decoding == 1)
        def _():
            for copy in memory_copies[side]:
                copy.start()

        for k in range(side * chunks // 2, (side + 1) * chunks // 2):
            for j in range(3):
                weight_copy(j, k).start()
    for k in range(chunks):
        weight_copy(3, k).start()

    for k in range(chunks):
        if k % (chunks // 2) == 0:
            side = k // (chunks // 2)
            for copy in pair_copies[side]:
                copy.wait()

            @pl.when(decoding == 1)
            def _():
                for copy in memory_copies[side]:
                    copy.wait()

        for j in range(3):
            weight_copy(j, k).wait()
        columns = pl.ds(k * chunk, chunk)
        for j in range(3):
            rows = source[0, :, columns] if j == 0 else source[decoding, :, columns]
            part = jnp.dot(rows, held[j, columns, :], preferred_element_type=jnp.float32)
            if k == 0:
                total[j] = part
            else:
                total[j] += part

    allowed = query_segs[...] == key_segs[...]
    lane = lax.broadcasted_iota(jnp.int32, (1, 2 * HEAD_DIM), 1)
    for two in range(width // (2 * HEAD_DIM)):
        lanes = pl.ds(two * 2 * HEAD_DIM, 2 * HEAD_DIM)
        queries = total[0, :, lanes].astype(jnp.bfloat16)
        key_rows = total[1, :, lanes].astype(jnp.bfloat16)
        value_rows = total[2, :, lanes].astype(jnp.bfloat16)
        mixed = None
        for head in range(2):
            here = (lane // HEAD_DIM) == head
            one = jnp.where(here, queries, jnp.zeros_like(queries))
            scores = lax.dot_general(
                one, key_rows, (((1,), (1,)), ((), ())), preferred_element_type=jnp.float32
            )
            masked = jnp.where(allowed, scores, -1e30)
            highest = jnp.max(masked, axis=-1, keepdims=True)
            powers = jnp.where(allowed, jnp.exp(masked - highest), 0.0)
            shares = (powers / jnp.sum(powers, axis=-1, keepdims=True)).astype(jnp.bfloat16)
            result = jnp.dot(shares, value_rows, preferred_element_type=jnp.float32)
            mixed = result if head == 0 else jnp.where(here, result, mixed)
        attended[:, lanes] = mixed.astype(jnp.bfloat16)

    def out_copy(i, other, side):
        rows = pl.ds(row(offsets[i], other), 32)
        return pltpu.make_async_copy(
            partial.at[rows, halves[side]], outs[2 * i + other].at[:, halves[side]], out_sems.at[side, 2 * i + other]
        )

    out_copies = [[out_copy(i, other, side) for i in range(8) for other in range(2)] for side in range(2)]
    for k in range(chunks):
        weight_copy(3, k).wait()
        columns = pl.ds(k * chunk, chunk)
        partial[:, columns] = lax.dot_general(
            attended[...], held[3, columns, :], (((1,), (1,)), ((), ())), preferred_element_type=jnp.float32
        ).astype(jnp.bfloat16)
        if (k + 1) % (chunks // 2) == 0:
            for copy in out_copies[k // (chunks // 2)]:
                copy.start()
    for copy in out_copies[0] + out_copies[1]:
        copy.wait()


def layer(place, pairs, memories, weight, query_segs, key_segs):
    width = pairs[0].shape[1]
    tokens = query_segs.shape[0]
    anywhere = pl.BlockSpec(memory_space=pl.ANY)
    inside = pl.BlockSpec(memory_space=pltpu.VMEM)
    return pl.pallas_call(
        layer_kernel,
        out_shape=[jax.ShapeDtypeStruct((32, width), jnp.bfloat16)] * 16,
        in_specs=[pl.BlockSpec(memory_space=pltpu.SMEM)] + [anywhere] * 25 + [inside] * 2,
        out_specs=[anywhere] * 16,
        scratch_shapes=[
            pltpu.VMEM((2, tokens, width), jnp.bfloat16),
            pltpu.VMEM(weight.shape, jnp.bfloat16),
            pltpu.VMEM((3, tokens, weight.shape[2]), jnp.float32),
            pltpu.VMEM((tokens, weight.shape[2]), jnp.bfloat16),
            pltpu.VMEM((tokens, width), jnp.bfloat16),
            pltpu.SemaphoreType.DMA((2, 16)),
            pltpu.SemaphoreType.DMA((2, 4)),
            pltpu.SemaphoreType.DMA((4, 4)),
            pltpu.SemaphoreType.DMA((2, 16)),
        ],
        compiler_params=pltpu.CompilerParams(vmem_limit_bytes=60 * 1024 * 1024),
        cost_estimate=pl.CostEstimate(flops=7_000_000_000, bytes_accessed=20_000_000, transcendentals=1_000_000),
    )(place, *pairs, *memories, weight, query_segs, key_segs)


def gradient_kernel(logits, log_total, wanted, first, second, out, rows, slopes, sems):
    vocab, half = slopes.shape[1:]
    copies = [pltpu.make_async_copy(a, rows.at[i], sems.at[i]) for i, a in enumerate((first, second))]
    for copy in copies:
        copy.start()
    entry = lax.broadcasted_iota(jnp.int32, (vocab, half), 0)
    for i in range(2):
        owned = (entry == wanted[i : i + 1, :]).astype(jnp.float32)
        slopes[i] = (jnp.exp(logits[i] - log_total[i : i + 1, :]) - owned).astype(jnp.bfloat16)
    for copy in copies:
        copy.wait()
    chunk = 1024
    for k in range(out.shape[1] // chunk):
        columns = pl.ds(k * chunk, chunk)
        out[:, columns] = sum(
            jnp.dot(slopes[i], rows[i, :, columns], preferred_element_type=jnp.float32) for i in range(2)
        )


def gradient(logits, log_total, wanted, first, second):
    anywhere = pl.BlockSpec(memory_space=pl.ANY)
    inside = pl.BlockSpec(memory_space=pltpu.VMEM)
    return pl.pallas_call(
        gradient_kernel,
        out_shape=jax.ShapeDtypeStruct((logits.shape[1], first.shape[1]), jnp.float32),
        in_specs=[inside] * 3 + [anywhere] * 2,
        out_specs=inside,
        scratch_shapes=[
            pltpu.VMEM((2,) + first.shape, jnp.bfloat16),
            pltpu.VMEM(logits.shape, jnp.bfloat16),
            pltpu.SemaphoreType.DMA((2,)),
        ],
        compiler_params=pltpu.CompilerParams(vmem_limit_bytes=32 * 1024 * 1024),
        cost_estimate=pl.CostEstimate(flops=540_000_000, bytes_accessed=7_000_000, transcendentals=66_000),
    )(logits, log_total, wanted, first, second)


def spread_final(rows):
    half = rows.shape[0] // 2
    plane = lax.axis_index("y") * 2 + lax.axis_index("xh")
    top, bottom = rows[:half], rows[half:]
    here = lax.ppermute(top, SECTION, [(15, 14)])
    moved = [lax.ppermute(top, SECTION, [(15, 12)]), lax.ppermute(bottom, SECTION, [(15, 13)])]
    last = lax.axis_index("c") == 1
    mine = jnp.where(plane == 6, jnp.where(last, moved[1], moved[0]), jnp.where(last, bottom, here))
    first = lax.ppermute(mine, ("y", "xh"), [(7, 5), (6, 4)])
    second = lax.ppermute(mine, ("y", "xh"), [(7, 1), (6, 0)])
    third = lax.ppermute(mine, ("y", "xh"), [(7, 3), (6, 2)])
    return jnp.where(plane >= 6, mine, jnp.where(plane >= 4, first, jnp.where(plane < 2, second, third)))


def join(highest, total, picked):
    top = jnp.max(highest, axis=0)
    return jnp.stack([top, jnp.sum(total * jnp.exp(highest - top), axis=0), jnp.sum(picked, axis=0)])


def combine(stats, axis):
    count = lax.axis_size(axis)
    every = lax.all_to_all(jnp.broadcast_to(stats[None], (count,) + stats.shape), axis, 0, 0)
    return join(every[:, 0], every[:, 1], every[:, 2])


def per_device(
    states, section_segs, weights, gains, memory, memory_segs, final_gain, embedding, targets
):
    section_index = lax.axis_index(SECTION)
    core = lax.axis_index("c")
    z = lax.axis_index("z")
    column = lax.axis_index("xl")
    sign = 1 - 2 * (z % 2)
    current = states[0]
    normed = norm_rows(current, gains[0]).astype(jnp.bfloat16)

    moves = [(0, 1), (1, 0), (1, 1)]
    routes = [[(i, i ^ (2 * a + b)) for i in range(4)] for a, b in moves]

    def memory_ring(step, known):
        if step == 0:
            rows = jnp.concatenate([memory] + [lax.ppermute(memory, ("xh", "xl"), route) for route in routes], axis=0)
            return (jnp.concatenate([rows] + [shift(rows, "y", d) for d in (1, 2, 3)], axis=0),)
        ahead, behind = (known * 2)[:2] if step == 1 else known[-2:]
        return known + (inner(behind), outer(ahead))

    found, near = gather_blocks(normed, memory_ring, settle=True)
    pairs = [block for pair in found for block in pair]
    half = normed.shape[1] // 2
    far = [inner(near[-1][:, :half]), outer(near[-2][:, half:])]
    mine = [join_rows(near)] + far
    memories = mine + [shift(block, "c", 1) for block in mine]
    query_segs = jnp.swapaxes(section_segs[0].reshape(2, 8, 32), 0, 1).reshape(-1)
    decoding = (section_index >= 8).astype(jnp.int32)
    key_segs = jnp.where(decoding == 1, pick(memory_segs, memory_rows()), query_segs)
    place = jnp.stack([z, sign, column, decoding]).astype(jnp.int32)
    parts = layer(place, pairs, memories, weights[0], query_segs[:, None], key_segs[None, :])
    summed = scatter_blocks(parts[0::2], parts[1::2])
    updated = (current.astype(jnp.float32) + summed).astype(jnp.bfloat16)
    spread = spread_final(norm_rows(updated, final_gain).astype(jnp.bfloat16))
    forward = [(i, i + 1) for i in range(15) if i != 7]
    gathered, (next_states,) = gather_blocks(
        spread, lambda step, known: (lax.ppermute(updated[None], SECTION, forward),) if step == 1 else known
    )

    offsets = [0, sign, -sign, 2 * sign, -2 * sign, 3 * sign, -3 * sign, 4]
    far = [jnp.concatenate([gathered[7][i], gathered[8][i]], axis=1) for i in range(2)]
    rows = jnp.zeros((8, 2) + spread.shape, spread.dtype)
    for offset, pair in zip(offsets, gathered[:7] + [far]):
        for i in range(2):
            rows = lax.dynamic_update_slice(
                rows, pair[i][None, None], ((z + 8 + offset) % 8, column if i == 0 else 1 - column, 0, 0)
            )
    held = rows.reshape(256, -1)
    halves = [held, shift(held, "c", 1)]

    def flip(value):
        return jnp.where(core == 1, value[..., ::-1, :], value)

    at = jnp.arange(512, dtype=jnp.int32)
    tokens = (at // 16 % 2) * 256 + (at // 32 % 8) * 32 + (core ^ (at // 256)) * 16 + at % 16
    vocab_local = embedding.shape[0]
    vocab_start = (section_index * 16 + lax.axis_index(MP)) * vocab_local
    wanted = (pick(targets, tokens) - vocab_start).reshape(2, 256)
    logits = jnp.stack(
        [
            lax.dot_general(embedding, half, (((1,), (1,)), ((), ())), preferred_element_type=jnp.float32)
            for half in halves
        ]
    )
    owned = wanted[:, None, :] == jnp.arange(vocab_local, dtype=jnp.int32)[None, :, None]
    local_max = jnp.max(logits, axis=1)
    local_sum = jnp.sum(jnp.exp(logits - local_max[:, None]), axis=1)
    picked = jnp.sum(jnp.where(owned, logits, 0.0), axis=1)
    stats = flip(jnp.stack([local_max, local_sum, picked]))
    stats = combine(combine(stats, MP), SECTION)
    log_total = stats[0] + jnp.log(stats[1])
    loss = (log_total - stats[2]).reshape(2, 8, 2, 16).transpose(2, 1, 0, 3).reshape(-1)
    embed_grad = gradient(logits, flip(log_total), wanted, *halves)
    return (next_states, loss, embed_grad)


def solution(mesh):
    fine = Mesh(mesh.devices.reshape(4, 2, 2, 2, 8), ("y", "xh", "c", "xl", "z"))
    everything = P(SECTION + MP, None)
    placed = (
        P(SECTION, MP, None),
        P(SECTION, None),
        P(SECTION, None, None, MP),
        P(SECTION, None),
        everything,
        P(),
        P(),
        everything,
        P(),
    )
    return jax.shard_map(
        per_device,
        mesh=fine,
        in_specs=placed,
        out_specs=(P(SECTION, MP, None), P(), everything),
        check_vma=False,
    )
```
